32 devices in a mesh: section: 8 (over z, core), tensor: 4 (over y, x).
Axes of the slice: x: 2, y: 2, z: 4, core: 2. Of those that a mesh axis runs over, the one named last changes fastest.
Arguments:
- section_inputs: bfloat16 [8, 2, 8192, 128], P('section', None, 'tensor'), may hold values from -6 to 6
- arriving_grad: bfloat16 [8, 8192, 128], P('section', 'tensor'), may hold values from -1.5 to 1.5
- loss_grad: bfloat16 [1, 8192, 128], P(None, 'tensor'), may hold values from -1.5 to 1.5
- factor_first: bfloat16 [8, 3, 64, 128, 128], P('section', None, 'tensor'), may hold values from -0.5 to 0.5
- factor_second: bfloat16 [8, 3, 64, 128, 128], P('section', None, 'tensor'), may hold values from -0.5 to 0.5
- gate_scales: float32 [8, 3, 8192], P('section', None, 'tensor'), may hold values from 0.25 to 1.5
- layer_count: int32 [8], P('section'), may hold values from 1 to 3, as said below
Outputs:
- last_emitted: bfloat16 [8, 8192, 128], P('section', 'tensor')
- factor_first_grad: bfloat16 [8, 3, 64, 128, 128], P('section', None, 'tensor')
- factor_second_grad: bfloat16 [8, 3, 64, 128, 128], P('section', None, 'tensor')
- gate_grad: float32 [8, 3, 8192], P('section', None, 'tensor')
The draws below stay inside these ranges and needn't reach their ends.
Inputs may be any that keep to these rules, and one draw needn't show every extreme that they name: `layer_count`: every section runs at least one layer and some section runs 3.
All inputs are finite; a program needn't handle non-finite values.
Results may differ from the reference program's by a relative error of at most 0.017.
Values may be sent and summed in bfloat16 or wider, within the bound.
A program may use at most 64 MiB of HBM per device.

```python
import jax
import jax.numpy as jnp
from jax import lax

NB = 64
BS = 128
D = 8192
LMAX = 3
TICKS = 2
TOK = 128
SECTIONS = 8


def draw_layer_count(key, part):
    first_key, second_key = jax.random.split(key)
    counts = jax.random.randint(first_key, (SECTIONS,), 1, 3)
    heavy_sections = jax.random.permutation(second_key, SECTIONS)[:SECTIONS // 16 + 1]
    counts = counts.at[heavy_sections].set(LMAX)
    return counts.astype(jnp.int32)


def block_scale(stream_key, extent, shards, low, high):
    factor_of, own = 1.0, jax.random.fold_in(stream_key, 6)
    for position, shards_of in shards:
        steps = jnp.exp(jax.random.uniform(jax.random.fold_in(own, position), (shards_of,), jnp.float32, low / len(shards), high / len(shards)))
        factor_of = factor_of * jnp.repeat(steps, extent[position] // shards_of).reshape([-1 if axis == position else 1 for axis in range(len(extent))])
    return factor_of


def noise(rng, shape, deviation, bound, cuts=(), dtype=jnp.bfloat16):
    factor_of = block_scale(rng, shape, cuts, -0.22, 0.18) if cuts else 1.0
    array = jax.random.normal(rng, shape, jnp.float32) * deviation * factor_of
    return jnp.minimum(jnp.maximum(array, -bound), bound).astype(dtype)


def setup_inputs(seed: int = 0) -> dict:
    seeds = jax.random.split(jax.random.key(seed), 8)
    section_inputs = noise(seeds[0], (SECTIONS, TICKS, D, TOK), 1.0, 6.0, ((0, 8), (2, 4)))
    arriving_grad = noise(seeds[1], (SECTIONS, D, TOK), 0.25, 1.5, ((0, 8), (1, 4)))
    loss_grad = noise(seeds[2], (TICKS - 1, D, TOK), 0.25, 1.5, ((1, 4),))
    factor_first = noise(seeds[3], (SECTIONS, LMAX, NB, BS, BS), BS ** -0.5, 0.5, ((0, 8), (2, 4)))
    factor_second = noise(seeds[4], (SECTIONS, LMAX, NB, BS, BS), BS ** -0.5, 0.5, ((0, 8), (2, 4)))
    gate_scales = jnp.clip(0.25 + 1.25 * jax.random.uniform(seeds[5], (SECTIONS, LMAX, D), jnp.float32) ** block_scale(seeds[5], (SECTIONS, LMAX, D), ((0, 8), (2, 4)), -0.2, 0.2), 0.25, 1.5)
    layer_count = draw_layer_count(jax.random.fold_in(seeds[7], 71), 0)
    return dict(section_inputs=section_inputs, arriving_grad=arriving_grad, loss_grad=loss_grad, factor_first=factor_first, factor_second=factor_second, gate_scales=gate_scales, layer_count=layer_count)


def permute_blocks(values):
    blocks_all = values.shape[0]
    repeat_count = values.shape[1] // blocks_all
    grid = values.reshape(blocks_all, blocks_all, repeat_count, -1).transpose(1, 2, 0, 3)
    return grid.reshape(blocks_all, blocks_all * repeat_count, -1)


def unpermute_blocks(values):
    blocks_all = values.shape[0]
    repeat_count = values.shape[1] // blocks_all
    grid = values.reshape(blocks_all, repeat_count, blocks_all, -1).transpose(2, 0, 1, 3)
    return grid.reshape(blocks_all, blocks_all * repeat_count, -1)


def apply_blocks(factor, values):
    return jnp.einsum("kij,kjt->kit", factor.astype(jnp.float32), values.astype(jnp.float32))


def apply_transposed(factor, values):
    return jnp.einsum("kji,kjt->kit", factor.astype(jnp.float32), values.astype(jnp.float32))


def section_backward(initial, grad_in, factor_one, factor_two, gate_rows, layer_total):
    hidden = initial.reshape(NB, BS, TOK)
    saved = []
    for layer_slot in range(LMAX):
        first_out = apply_blocks(factor_one[layer_slot], hidden).astype(jnp.bfloat16)
        permuted = permute_blocks(first_out)
        mixed = apply_blocks(factor_two[layer_slot], permuted)
        gate_now = gate_rows[layer_slot].reshape(NB, BS, 1)
        next_hidden = (hidden.astype(jnp.float32) + gate_now * (mixed * jax.nn.sigmoid(mixed))).astype(jnp.bfloat16)
        saved.append((hidden, permuted, mixed))
        hidden = jnp.where(layer_slot < layer_total, next_hidden, hidden)
    grad_now = grad_in.reshape(NB, BS, TOK).astype(jnp.float32)
    first_terms = [None] * LMAX
    second_terms = [None] * LMAX
    gate_terms = [None] * LMAX
    for layer_slot in reversed(range(LMAX)):
        hidden, permuted, mixed = saved[layer_slot]
        is_live = layer_slot < layer_total
        logistic = jax.nn.sigmoid(mixed)
        gate_now = gate_rows[layer_slot].reshape(NB, BS, 1)
        gate_term = jnp.sum(grad_now * (mixed * logistic), axis=2)
        scaled = (grad_now * gate_now * logistic * (1.0 + mixed * (1.0 - logistic))).astype(jnp.bfloat16)
        backed = apply_transposed(factor_two[layer_slot], scaled).astype(jnp.bfloat16)
        returned = unpermute_blocks(backed)
        second_term = jnp.einsum("kit,kjt->kij", scaled.astype(jnp.float32), permuted.astype(jnp.float32))
        first_term = jnp.einsum("kit,kjt->kij", returned.astype(jnp.float32), hidden.astype(jnp.float32))
        moved_grad = grad_now + apply_transposed(factor_one[layer_slot], returned)
        grad_now = jnp.where(is_live, moved_grad, grad_now)
        first_terms[layer_slot] = jnp.where(is_live, first_term, jnp.zeros_like(first_term))
        second_terms[layer_slot] = jnp.where(is_live, second_term, jnp.zeros_like(second_term))
        gate_terms[layer_slot] = jnp.where(is_live, gate_term, jnp.zeros_like(gate_term)).reshape(NB * BS)
    emitted = grad_now.astype(jnp.bfloat16).reshape(NB * BS, TOK)
    return emitted, jnp.stack(first_terms), jnp.stack(second_terms), jnp.stack(gate_terms)


def reference(section_inputs, arriving_grad, loss_grad, factor_first, factor_second, gate_scales, layer_count):
    def emit_only(section_item):
        return section_backward(*section_item)[0]

    grad_list = []
    emitted = None
    for moment in range(TICKS):
        if moment == 0:
            arriving = arriving_grad
        else:
            arriving = jnp.concatenate([emitted[1:], loss_grad[moment - 1][None]], axis=0)
        grad_list.append(arriving)
        emitted = lax.map(emit_only, (section_inputs[:, moment], arriving, factor_first, factor_second, gate_scales, layer_count))
    arrivals = jnp.stack(grad_list, axis=1)

    def section_grads(section_item):
        section_acts, section_arrivals, first_section, second_section, gate_section, total_section = section_item
        sums = None
        for moment in range(TICKS):
            fresh = section_backward(section_acts[moment], section_arrivals[moment], first_section, second_section, gate_section, total_section)[1:]
            if sums is None:
                sums = fresh
            else:
                sums = tuple(older + newer for older, newer in zip(sums, fresh))
        return sums[0].astype(jnp.bfloat16), sums[1].astype(jnp.bfloat16), sums[2]

    first_grad, second_grad, gate_grad = lax.map(section_grads, (section_inputs, arrivals, factor_first, factor_second, gate_scales, layer_count))
    return emitted, first_grad, second_grad, gate_grad
```

```python
import functools

import jax
import jax.numpy as jnp
from jax import lax
from jax.experimental import pallas as pl
from jax.experimental.pallas import tpu as pltpu
from jax.sharding import PartitionSpec as P


def from_behind(value, axis, steps):
    count = lax.axis_size(axis)
    initial, last = (max(0, -steps), min(count, count - steps))
    return lax.ppermute(value, axis, [(source, source + steps) for source in range(initial, last)])


def permute_blocks(values):
    tensor_size = lax.axis_size("tensor")
    batch_count, local_blocks, block_size, token_count = values.shape
    blocks_all = local_blocks * tensor_size
    repeat_count = block_size // blocks_all
    shaped = values.reshape(
        batch_count, local_blocks, tensor_size, local_blocks, repeat_count, token_count
    )
    moved = lax.all_to_all(shaped, "tensor", split_axis=2, concat_axis=1, tiled=True)
    moved = moved.reshape(batch_count, blocks_all, local_blocks, repeat_count, token_count)
    return moved.transpose(0, 2, 3, 1, 4).reshape(
        batch_count, local_blocks, block_size, token_count
    )


def unpermute_blocks(values):
    tensor_size = lax.axis_size("tensor")
    local_blocks, block_size, token_count = values.shape
    blocks_all = local_blocks * tensor_size
    repeat_count = block_size // blocks_all
    shaped = values.reshape(local_blocks, repeat_count, tensor_size, local_blocks, token_count)
    moved = lax.all_to_all(shaped, "tensor", split_axis=2, concat_axis=0, tiled=True)
    moved = moved.reshape(blocks_all, repeat_count, local_blocks, token_count)
    return moved.transpose(2, 0, 1, 3).reshape(local_blocks, block_size, token_count)


def recompute(initial, factor_one, factor_two, gate_rows, layer_total):
    slot_count = factor_one.shape[0]
    hidden = initial
    saved = []
    for layer_slot in range(slot_count):
        first_out = jnp.einsum(
            "kij,mkjt->mkit", factor_one[layer_slot], hidden, preferred_element_type=jnp.float32
        ).astype(jnp.bfloat16)
        permuted = permute_blocks(first_out)
        mixed = jnp.einsum(
            "kij,mkjt->mkit", factor_two[layer_slot], permuted, preferred_element_type=jnp.float32
        )
        gate_now = gate_rows[layer_slot][None, :, :, None]
        next_hidden = (
            hidden.astype(jnp.float32) + gate_now * (mixed * jax.nn.sigmoid(mixed))
        ).astype(jnp.bfloat16)
        saved.append((hidden, permuted, mixed))
        hidden = jnp.where(layer_slot < layer_total, next_hidden, hidden)
    return saved


def shards(
    section_inputs, arriving_grad, loss_grad, factor_first, factor_second, gate_scales, layer_count
):
    moments = section_inputs.shape[1]
    slot_count = factor_first.shape[1]
    local_blocks = factor_first.shape[2]
    block_size = factor_first.shape[3]
    token_count = section_inputs.shape[3]
    first_local = factor_first[0]
    second_local = factor_second[0]
    gate_rows = gate_scales[0].reshape(slot_count, local_blocks, block_size)
    layer_total = layer_count[0]
    section_id = lax.axis_index("section")
    last_section = lax.axis_size("section") - 1
    inputs_local = section_inputs[0].reshape(moments, local_blocks, block_size, token_count)
    first_acc = [
        jnp.zeros((local_blocks, block_size, block_size), jnp.float32) for slot in range(slot_count)
    ]
    second_acc = [
        jnp.zeros((local_blocks, block_size, block_size), jnp.float32) for slot in range(slot_count)
    ]
    gate_acc = [jnp.zeros((local_blocks, block_size), jnp.float32) for slot in range(slot_count)]
    emitted = None
    for moment in range(moments):
        if moment == 0:
            arrived = arriving_grad[0].reshape(local_blocks, block_size, token_count)
        else:
            shifted = from_behind(emitted, "section", -1)
            from_loss = loss_grad[moment - 1].reshape(local_blocks, block_size, token_count)
            arrived = jnp.where(section_id == last_section, from_loss, shifted)
        computed = recompute(
            inputs_local[moment : moment + 1], first_local, second_local, gate_rows, layer_total
        )
        saved = [(record[0][0], record[1][0], record[2][0]) for record in computed]
        grad_now = arrived.astype(jnp.float32)
        for layer_slot in reversed(range(slot_count)):
            hidden, permuted, mixed = saved[layer_slot]
            is_live = layer_slot < layer_total
            logistic = jax.nn.sigmoid(mixed)
            gate_now = gate_rows[layer_slot][:, :, None]
            gate_term = jnp.sum(grad_now * (mixed * logistic), axis=2)
            gate_acc[layer_slot] = gate_acc[layer_slot] + jnp.where(
                is_live, gate_term, jnp.zeros_like(gate_term)
            )
            scaled = (grad_now * gate_now * logistic * (1.0 + mixed * (1.0 - logistic))).astype(
                jnp.bfloat16
            )
            backed = jnp.einsum(
                "kji,kjt->kit", second_local[layer_slot], scaled, preferred_element_type=jnp.float32
            ).astype(jnp.bfloat16)
            returned = unpermute_blocks(backed)
            moved_grad = grad_now + jnp.einsum(
                "kji,kjt->kit",
                first_local[layer_slot],
                returned,
                preferred_element_type=jnp.float32,
            )
            grad_now = jnp.where(is_live, moved_grad, grad_now)
            second_term = jnp.einsum(
                "kit,kjt->kij", scaled, permuted, preferred_element_type=jnp.float32
            )
            first_term = jnp.einsum(
                "kit,kjt->kij", returned, hidden, preferred_element_type=jnp.float32
            )
            second_acc[layer_slot] = second_acc[layer_slot] + jnp.where(
                is_live, second_term, jnp.zeros_like(second_term)
            )
            first_acc[layer_slot] = first_acc[layer_slot] + jnp.where(
                is_live, first_term, jnp.zeros_like(first_term)
            )
        emitted = grad_now.astype(jnp.bfloat16)
    last_emitted = emitted.reshape(1, local_blocks * block_size, token_count)
    gate_out = jnp.stack(gate_acc).reshape(1, slot_count, local_blocks * block_size)
    first_out = jnp.stack(first_acc).astype(jnp.bfloat16)[None]
    second_out = jnp.stack(second_acc).astype(jnp.bfloat16)[None]
    return (last_emitted, first_out, second_out, gate_out)


MESH = pl.DeviceIdType.MESH
F32 = jnp.float32
BF16 = jnp.bfloat16
CHUNKS = 4


def kernel(
    inp, arr, loss, one, two, gate, count_ref,
    emit_out, first_out, second_out, gate_out,
    hid, perm, ret, send_f, send_b, work, slope, silu, gate_b, grad, gate_acc, scaled,
    hop_in, hop_out,
    recv_f, recv_b, sent_f, sent_b, hop_recv, hop_sent, loss_sem,
):
    slots, blocks, size, tokens = one.shape
    rows = perm.shape[1]
    repeat = rows // blocks
    per = blocks // CHUNKS
    span = rows // CHUNKS
    me = lax.axis_index("tensor")
    section = lax.axis_index("section")
    last = lax.axis_size("section") - 1
    me_low, me_high = me % 2, me // 2

    def partner(d):
        low = 1 - me_low if d % 2 else me_low
        high = 1 - me_high if d // 2 else me_high
        return high * 2 + low

    barrier = pltpu.get_barrier_semaphore()
    for d in (1, 2, 3):
        pl.semaphore_signal(
            barrier, inc=1, device_id={"tensor": partner(d)}, device_id_type=MESH
        )

    @pl.when(section > 0)
    def _():
        pl.semaphore_signal(barrier, inc=1, device_id={"section": section - 1}, device_id_type=MESH)

    @pl.when(section < last)
    def _():
        pl.semaphore_signal(barrier, inc=1, device_id={"section": section + 1}, device_id_type=MESH)

    @pl.when(section == last)
    def _():
        pltpu.make_async_copy(loss, hop_in, loss_sem).start()

    count = count_ref[0]

    def hidden(t, l):
        return inp.at[t] if l == 0 else hid.at[t, l - 1]

    def step(t, l):
        return t * slots + l

    def dot(a, b):
        return jnp.dot(a, b, preferred_element_type=F32)

    def dot_t(a, b):
        return lax.dot_general(a, b, (((0,), (0,)), ((), ())), preferred_element_type=F32)

    def work_rows(k):
        return pl.ds(pl.multiple_of(k * size, size), size)

    def each_chunk(body):
        lax.fori_loop(0, CHUNKS, lambda c, _: (body(c), 0)[1], 0)

    def each_block(body):
        def chunk(c):
            for b in range(per):
                body(c * per + b)

        each_chunk(chunk)

    def copy_f(f, d, c, source):
        part = pl.ds(c * span, span)
        return pltpu.make_async_remote_copy(
            src_ref=send_f.at[f, d - 1, part],
            dst_ref=perm.at[f, part, source],
            send_sem=sent_f.at[f, d - 1],
            recv_sem=recv_f.at[f, c, d - 1],
            device_id={"tensor": partner(d)},
            device_id_type=MESH,
        )

    def copy_b(f, d, c, source):
        part = pl.ds(c * per, per)
        return pltpu.make_async_remote_copy(
            src_ref=send_b.at[f, d - 1, part],
            dst_ref=ret.at[f, part, source],
            send_sem=sent_b.at[f, d - 1],
            recv_sem=recv_b.at[f, c, d - 1],
            device_id={"tensor": partner(d)},
            device_id_type=MESH,
        )

    def scatter_f(f):
        def chunk(c):
            for d in (3, 1, 2, 0):
                target = partner(d)
                for j in range(span):
                    row = c * span + j
                    tile = work[pl.ds(target * rows + row, blocks, stride=size), :].astype(BF16)
                    if d:
                        send_f[f, d - 1, row] = tile
                    else:
                        perm[f, row, me] = tile
                if d:
                    copy_f(f, d, c, me).start()

        each_chunk(chunk)

    def scatter_b(f):
        def chunk(c):
            for d in (3, 1, 2, 0):
                target = partner(d)
                for j in range(per):
                    block = c * per + j
                    tile = work[
                        pl.ds(target * blocks + block, rows, stride=size // repeat), :
                    ].astype(BF16)
                    if d:
                        send_b[f, d - 1, block] = tile
                    else:
                        ret[f, block, me] = tile
                if d:
                    copy_b(f, d, c, me).start()

        each_chunk(chunk)

    def permuted(f, k):
        return perm[f, pl.ds(k * repeat, repeat)].reshape(size, tokens)

    def back(t, l, k, value):
        f = step(t, l)
        rounded = (value * slope[f, k]).astype(BF16)
        scaled[f, k] = rounded
        work[work_rows(k), :] = dot_t(two[l, k], rounded)
        grad[k] = value
        product = value * silu[f, k]
        gate_acc[l, k] = product if t == 0 else gate_acc[l, k] + product

    def forward(t, l, then):
        f = step(t, l)

        def chunk(c):
            for d in (1, 2, 3):
                copy_f(f, d, c, partner(d)).wait_recv()
            for b in range(per):
                k = c * per + b
                mixed = dot(two[l, k], permuted(f, k))
                logistic = 0.5 + 0.5 * jnp.tanh(0.5 * mixed)
                branch = mixed * logistic
                scale = gate_b[l, k]
                if l + 1 < slots:
                    old = hidden(t, l)[k].astype(F32)
                    new = jnp.where(l < count, old + scale * branch, old).astype(BF16)
                    hid[t, l, k] = new
                    work[work_rows(k), :] = dot(one[l + 1, k], new)
                silu[f, k] = branch
                slope[f, k] = scale * (logistic * (1.0 + mixed * (1.0 - logistic)))
                if then is not None:
                    then(k)

        each_chunk(chunk)

    def backward(t, l, then):
        f = step(t, l)

        def chunk(c):
            for d in (1, 2, 3):
                copy_b(f, d, c, partner(d)).wait_recv()
            for b in range(per):
                k = c * per + b
                term = dot_t(one[l, k], ret[f, k].reshape(size, tokens))
                value = jnp.where(l < count, grad[k] + term, grad[k])
                then(k, value)
            if t == 0 and l == 0:
                hop_send(c)

        each_chunk(chunk)

    def hop_copy(c):
        part = pl.ds(c * per, per)
        return pltpu.make_async_remote_copy(
            src_ref=hop_out.at[part],
            dst_ref=hop_in.at[part],
            send_sem=hop_sent.at[c],
            recv_sem=hop_recv.at[c],
            device_id={"section": section - 1},
            device_id_type=MESH,
        )

    def hop_send(c):
        @pl.when(section > 0)
        def _():
            hop_copy(c).start()

    def second_grads(l):
        f, g = step(0, l), step(1, l)

        def block(k):
            left = jnp.concatenate([scaled[f, k], scaled[g, k]], axis=1)
            right = jnp.concatenate([permuted(f, k), permuted(g, k)], axis=1)
            total = lax.dot_general(left, right, (((1,), (1,)), ((), ())), preferred_element_type=F32)
            second_out[l, k] = jnp.where(l < count, total, 0.0).astype(BF16)
            gates = jnp.sum(gate_acc[l, k].T, axis=0, keepdims=True)
            gate_out[l, pl.ds(k, 1), :] = jnp.where(l < count, gates, 0.0)

        each_block(block)

    def first_grads(l):
        f, g = step(0, l), step(1, l)

        def block(k):
            left = jnp.concatenate(
                [ret[f, k].reshape(size, tokens), ret[g, k].reshape(size, tokens)], axis=1
            )
            right = jnp.concatenate([hidden(0, l)[k], hidden(1, l)[k]], axis=1)
            total = lax.dot_general(left, right, (((1,), (1,)), ((), ())), preferred_element_type=F32)
            first_out[l, k] = jnp.where(l < count, total, 0.0).astype(BF16)

        each_block(block)

    def start(t):
        def block(k):
            work[work_rows(k), :] = dot(one[0, k], inp[t, k])

        each_block(block)

    def widen(l):
        def block(k):
            gate_b[l, k] = jnp.broadcast_to(gate[l, pl.ds(k, 1), :], (size, size)).T

        each_block(block)

    start(0)
    pl.semaphore_wait(
        barrier, 3 + jnp.where(section > 0, 1, 0) + jnp.where(section < last, 1, 0)
    )
    scatter_f(step(0, 0))
    start(1)
    scatter_f(step(1, 0))
    for l in range(slots):
        widen(l)
    top = slots - 1
    for l in range(top):
        for t in (0, 1):
            forward(t, l, None)
            scatter_f(step(t, l + 1))
    forward(0, top, lambda k: back(0, top, k, arr[k].astype(F32)))
    scatter_b(step(0, top))
    forward(1, top, None)
    for l in range(top, 0, -1):
        backward(0, l, functools.partial(back, 0, l - 1))
        scatter_b(step(0, l - 1))

    def leave(k, value):
        hop_out[k] = value.astype(BF16)

    backward(0, 0, leave)

    @pl.when(section == last)
    def _():
        pltpu.make_async_copy(loss, hop_in, loss_sem).wait()

    def arrive(c):
        @pl.when(section < last)
        def _():
            hop_copy(c).wait_recv()

        for b in range(per):
            k = c * per + b
            back(1, top, k, hop_in[k].astype(F32))

    each_chunk(arrive)
    scatter_b(step(1, top))
    for l in range(top, 0, -1):
        second_grads(l)
        if l < top:
            first_grads(l + 1)
        backward(1, l, functools.partial(back, 1, l - 1))
        scatter_b(step(1, l - 1))
    second_grads(0)
    if top > 0:
        first_grads(1)

    def emit(k, value):
        emit_out[k] = value.astype(BF16)

    backward(1, 0, emit)
    first_grads(0)

    for t in (0, 1):
        for l in range(slots):
            f = step(t, l)
            for d in (1, 2, 3):
                pltpu.make_async_remote_copy(
                    src_ref=send_f.at[f, d - 1], dst_ref=perm.at[f, :, me],
                    send_sem=sent_f.at[f, d - 1], recv_sem=recv_f.at[f, 0, d - 1],
                    device_id={"tensor": partner(d)}, device_id_type=MESH,
                ).wait_send()
                pltpu.make_async_remote_copy(
                    src_ref=send_b.at[f, d - 1], dst_ref=ret.at[f, :, me],
                    send_sem=sent_b.at[f, d - 1], recv_sem=recv_b.at[f, 0, d - 1],
                    device_id={"tensor": partner(d)}, device_id_type=MESH,
                ).wait_send()

    @pl.when(section > 0)
    def _():
        each_chunk(lambda c: hop_copy(c).wait_send())


def fused_shards(
    section_inputs, arriving_grad, loss_grad, factor_first, factor_second, gate_scales, layer_count
):
    moments = section_inputs.shape[1]
    _, slots, blocks, size, _ = factor_first.shape
    tokens = section_inputs.shape[3]
    tensor = lax.axis_size("tensor")
    rows = size // tensor
    steps = moments * slots
    vmem = pl.BlockSpec(memory_space=pltpu.VMEM)
    block = (blocks, size, tokens)
    factor = (slots, blocks, size, size)
    outs = pl.pallas_call(
        kernel,
        out_shape=[
            jax.ShapeDtypeStruct(block, BF16),
            jax.ShapeDtypeStruct(factor, BF16),
            jax.ShapeDtypeStruct(factor, BF16),
            jax.ShapeDtypeStruct((slots, blocks, size), F32),
        ],
        in_specs=[vmem] * 6 + [pl.BlockSpec(memory_space=pltpu.SMEM)],
        out_specs=[vmem] * 4,
        scratch_shapes=[
            pltpu.VMEM((moments, max(slots - 1, 1)) + block, BF16),
            pltpu.VMEM((steps, rows, tensor, blocks, tokens), BF16),
            pltpu.VMEM((steps, blocks, tensor, rows, tokens), BF16),
            pltpu.VMEM((steps, 3, rows, blocks, tokens), BF16),
            pltpu.VMEM((steps, 3, blocks, rows, tokens), BF16),
            pltpu.VMEM((blocks * size, tokens), F32),
            pltpu.VMEM((steps,) + block, F32),
            pltpu.VMEM((steps,) + block, F32),
            pltpu.VMEM((slots,) + block, F32),
            pltpu.VMEM(block, F32),
            pltpu.VMEM((slots,) + block, F32),
            pltpu.VMEM((steps,) + block, BF16),
            pltpu.VMEM(block, BF16),
            pltpu.VMEM(block, BF16),
            pltpu.SemaphoreType.DMA((steps, CHUNKS, 3)),
            pltpu.SemaphoreType.DMA((steps, CHUNKS, 3)),
            pltpu.SemaphoreType.DMA((steps, 3)),
            pltpu.SemaphoreType.DMA((steps, 3)),
            pltpu.SemaphoreType.DMA((CHUNKS,)),
            pltpu.SemaphoreType.DMA((CHUNKS,)),
            pltpu.SemaphoreType.DMA(()),
        ],
        compiler_params=pltpu.CompilerParams(
            collective_id=0, has_side_effects=True, vmem_limit_bytes=56 * 1024 * 1024
        ),
    )(
        section_inputs[0].reshape((moments,) + block),
        arriving_grad[0].reshape(block),
        loss_grad[0].reshape(block),
        factor_first[0],
        factor_second[0],
        gate_scales[0].reshape(slots, blocks, size),
        layer_count,
    )
    emitted, first_grad, second_grad, gate_grad = outs
    return (
        emitted.reshape(1, blocks * size, tokens),
        first_grad[None],
        second_grad[None],
        gate_grad.reshape(1, slots, blocks * size),
    )


def solution(mesh):
    in_specs = (
        P("section", None, "tensor", None),
        P("section", "tensor", None),
        P(None, "tensor", None),
        P("section", None, "tensor", None, None),
        P("section", None, "tensor", None, None),
        P("section", None, "tensor"),
        P("section"),
    )
    out_specs = (
        P("section", "tensor", None),
        P("section", None, "tensor", None, None),
        P("section", None, "tensor", None, None),
        P("section", None, "tensor"),
    )
    fused = mesh.shape["tensor"] == 4
    return jax.shard_map(fused_shards if fused else shards, mesh=mesh, in_specs=in_specs, out_specs=out_specs, check_vma=False)
```

```python
import functools

import jax
import jax.numpy as jnp
from jax import lax
from jax.experimental import pallas as pl
from jax.experimental.pallas import tpu as pltpu
from jax.sharding import PartitionSpec as P


def from_behind(value, axis, steps):
    count = lax.axis_size(axis)
    initial, last = (max(0, -steps), min(count, count - steps))
    return lax.ppermute(value, axis, [(source, source + steps) for source in range(initial, last)])


def permute_blocks(values):
    tensor_size = lax.axis_size("tensor")
    batch_count, local_blocks, block_size, token_count = values.shape
    blocks_all = local_blocks * tensor_size
    repeat_count = block_size // blocks_all
    shaped = values.reshape(
        batch_count, local_blocks, tensor_size, local_blocks, repeat_count, token_count
    )
    moved = lax.all_to_all(shaped, "tensor", split_axis=2, concat_axis=1, tiled=True)
    moved = moved.reshape(batch_count, blocks_all, local_blocks, repeat_count, token_count)
    return moved.transpose(0, 2, 3, 1, 4).reshape(
        batch_count, local_blocks, block_size, token_count
    )


def unpermute_blocks(values):
    tensor_size = lax.axis_size("tensor")
    local_blocks, block_size, token_count = values.shape
    blocks_all = local_blocks * tensor_size
    repeat_count = block_size // blocks_all
    shaped = values.reshape(local_blocks, repeat_count, tensor_size, local_blocks, token_count)
    moved = lax.all_to_all(shaped, "tensor", split_axis=2, concat_axis=0, tiled=True)
    moved = moved.reshape(blocks_all, repeat_count, local_blocks, token_count)
    return moved.transpose(2, 0, 1, 3).reshape(local_blocks, block_size, token_count)


def recompute(initial, factor_one, factor_two, gate_rows, layer_total):
    slot_count = factor_one.shape[0]
    hidden = initial
    saved = []
    for layer_slot in range(slot_count):
        first_out = jnp.einsum(
            "kij,mkjt->mkit", factor_one[layer_slot], hidden, preferred_element_type=jnp.float32
        ).astype(jnp.bfloat16)
        permuted = permute_blocks(first_out)
        mixed = jnp.einsum(
            "kij,mkjt->mkit", factor_two[layer_slot], permuted, preferred_element_type=jnp.float32
        )
        gate_now = gate_rows[layer_slot][None, :, :, None]
        next_hidden = (
            hidden.astype(jnp.float32) + gate_now * (mixed * jax.nn.sigmoid(mixed))
        ).astype(jnp.bfloat16)
        saved.append((hidden, permuted, mixed))
        hidden = jnp.where(layer_slot < layer_total, next_hidden, hidden)
    return saved


def shards(
    section_inputs, arriving_grad, loss_grad, factor_first, factor_second, gate_scales, layer_count
):
    moments = section_inputs.shape[1]
    slot_count = factor_first.shape[1]
    local_blocks = factor_first.shape[2]
    block_size = factor_first.shape[3]
    token_count = section_inputs.shape[3]
    first_local = factor_first[0]
    second_local = factor_second[0]
    gate_rows = gate_scales[0].reshape(slot_count, local_blocks, block_size)
    layer_total = layer_count[0]
    section_id = lax.axis_index("section")
    last_section = lax.axis_size("section") - 1
    inputs_local = section_inputs[0].reshape(moments, local_blocks, block_size, token_count)
    first_acc = [
        jnp.zeros((local_blocks, block_size, block_size), jnp.float32) for slot in range(slot_count)
    ]
    second_acc = [
        jnp.zeros((local_blocks, block_size, block_size), jnp.float32) for slot in range(slot_count)
    ]
    gate_acc = [jnp.zeros((local_blocks, block_size), jnp.float32) for slot in range(slot_count)]
    emitted = None
    for moment in range(moments):
        if moment == 0:
            arrived = arriving_grad[0].reshape(local_blocks, block_size, token_count)
        else:
            shifted = from_behind(emitted, "section", -1)
            from_loss = loss_grad[moment - 1].reshape(local_blocks, block_size, token_count)
            arrived = jnp.where(section_id == last_section, from_loss, shifted)
        computed = recompute(
            inputs_local[moment : moment + 1], first_local, second_local, gate_rows, layer_total
        )
        saved = [(record[0][0], record[1][0], record[2][0]) for record in computed]
        grad_now = arrived.astype(jnp.float32)
        for layer_slot in reversed(range(slot_count)):
            hidden, permuted, mixed = saved[layer_slot]
            is_live = layer_slot < layer_total
            logistic = jax.nn.sigmoid(mixed)
            gate_now = gate_rows[layer_slot][:, :, None]
            gate_term = jnp.sum(grad_now * (mixed * logistic), axis=2)
            gate_acc[layer_slot] = gate_acc[layer_slot] + jnp.where(
                is_live, gate_term, jnp.zeros_like(gate_term)
            )
            scaled = (grad_now * gate_now * logistic * (1.0 + mixed * (1.0 - logistic))).astype(
                jnp.bfloat16
            )
            backed = jnp.einsum(
                "kji,kjt->kit", second_local[layer_slot], scaled, preferred_element_type=jnp.float32
            ).astype(jnp.bfloat16)
            returned = unpermute_blocks(backed)
            moved_grad = grad_now + jnp.einsum(
                "kji,kjt->kit",
                first_local[layer_slot],
                returned,
                preferred_element_type=jnp.float32,
            )
            grad_now = jnp.where(is_live, moved_grad, grad_now)
            second_term = jnp.einsum(
                "kit,kjt->kij", scaled, permuted, preferred_element_type=jnp.float32
            )
            first_term = jnp.einsum(
                "kit,kjt->kij", returned, hidden, preferred_element_type=jnp.float32
            )
            second_acc[layer_slot] = second_acc[layer_slot] + jnp.where(
                is_live, second_term, jnp.zeros_like(second_term)
            )
            first_acc[layer_slot] = first_acc[layer_slot] + jnp.where(
                is_live, first_term, jnp.zeros_like(first_term)
            )
        emitted = grad_now.astype(jnp.bfloat16)
    last_emitted = emitted.reshape(1, local_blocks * block_size, token_count)
    gate_out = jnp.stack(gate_acc).reshape(1, slot_count, local_blocks * block_size)
    first_out = jnp.stack(first_acc).astype(jnp.bfloat16)[None]
    second_out = jnp.stack(second_acc).astype(jnp.bfloat16)[None]
    return (last_emitted, first_out, second_out, gate_out)


MESH = pl.DeviceIdType.MESH
F32 = jnp.float32
BF16 = jnp.bfloat16
CHUNKS = 4


def kernel(
    inp_far, arr_far, loss, one_far, two_far, gate_far, count_ref,
    emit_out, first_out, second_out, gate_out,
    inp, arr, one, two, gate, hid, perm, ret, send_f, send_b, work, slope, silu, gate_b, grad, gate_acc, scaled,
    hop_in, hop_out,
    recv_f, recv_b, sent_f, sent_b, hop_recv, hop_sent, loss_sem,
    inp_sem, one_sem, two_sem, far_sem,
):
    slots, blocks, size, tokens = one.shape
    rows = perm.shape[1]
    repeat = rows // blocks
    per = blocks // CHUNKS
    span = rows // CHUNKS
    me = lax.axis_index("tensor")
    section = lax.axis_index("section")
    last = lax.axis_size("section") - 1
    me_low, me_high = me % 2, me // 2

    def partner(d):
        low = 1 - me_low if d % 2 else me_low
        high = 1 - me_high if d // 2 else me_high
        return high * 2 + low

    def load_inp(t):
        return pltpu.make_async_copy(inp_far.at[t], inp.at[t], inp_sem.at[t])

    def load_one(l):
        return pltpu.make_async_copy(one_far.at[l], one.at[l], one_sem.at[l])

    def load_two(l):
        return pltpu.make_async_copy(two_far.at[l], two.at[l], two_sem.at[l])

    load_gate = pltpu.make_async_copy(gate_far, gate, far_sem.at[0])
    load_arr = pltpu.make_async_copy(arr_far, arr, far_sem.at[1])
    load_inp(0).start()
    load_one(0).start()
    load_inp(1).start()
    load_gate.start()
    for l in range(slots):
        load_two(l).start()
        if l:
            load_one(l).start()
    load_arr.start()

    barrier = pltpu.get_barrier_semaphore()
    for d in (1, 2, 3):
        pl.semaphore_signal(
            barrier, inc=1, device_id={"tensor": partner(d)}, device_id_type=MESH
        )

    @pl.when(section > 0)
    def _():
        pl.semaphore_signal(barrier, inc=1, device_id={"section": section - 1}, device_id_type=MESH)

    @pl.when(section < last)
    def _():
        pl.semaphore_signal(barrier, inc=1, device_id={"section": section + 1}, device_id_type=MESH)

    @pl.when(section == last)
    def _():
        pltpu.make_async_copy(loss, hop_in, loss_sem).start()

    count = count_ref[0]

    def hidden(t, l):
        return inp.at[t] if l == 0 else hid.at[t, l - 1]

    def step(t, l):
        return t * slots + l

    def dot(a, b):
        return jnp.dot(a, b, preferred_element_type=F32)

    def dot_t(a, b):
        return lax.dot_general(a, b, (((0,), (0,)), ((), ())), preferred_element_type=F32)

    def work_rows(k):
        return pl.ds(pl.multiple_of(k * size, size), size)

    def each_chunk(body):
        lax.fori_loop(0, CHUNKS, lambda c, _: (body(c), 0)[1], 0)

    def each_block(body):
        def chunk(c):
            for b in range(per):
                body(c * per + b)

        each_chunk(chunk)

    def copy_f(f, d, c, source):
        part = pl.ds(c * span, span)
        return pltpu.make_async_remote_copy(
            src_ref=send_f.at[f, d - 1, part],
            dst_ref=perm.at[f, part, source],
            send_sem=sent_f.at[f, d - 1],
            recv_sem=recv_f.at[f, c, d - 1],
            device_id={"tensor": partner(d)},
            device_id_type=MESH,
        )

    def copy_b(f, d, c, source):
        part = pl.ds(c * per, per)
        return pltpu.make_async_remote_copy(
            src_ref=send_b.at[f, d - 1, part],
            dst_ref=ret.at[f, part, source],
            send_sem=sent_b.at[f, d - 1],
            recv_sem=recv_b.at[f, c, d - 1],
            device_id={"tensor": partner(d)},
            device_id_type=MESH,
        )

    def scatter_f(f):
        def chunk(c):
            for d in (3, 1, 2, 0):
                target = partner(d)
                for j in range(span):
                    row = c * span + j
                    tile = work[pl.ds(target * rows + row, blocks, stride=size), :].astype(BF16)
                    if d:
                        send_f[f, d - 1, row] = tile
                    else:
                        perm[f, row, me] = tile
                if d:
                    copy_f(f, d, c, me).start()

        each_chunk(chunk)

    def scatter_b(f):
        def chunk(c):
            for d in (3, 1, 2, 0):
                target = partner(d)
                for j in range(per):
                    block = c * per + j
                    tile = work[
                        pl.ds(target * blocks + block, rows, stride=size // repeat), :
                    ].astype(BF16)
                    if d:
                        send_b[f, d - 1, block] = tile
                    else:
                        ret[f, block, me] = tile
                if d:
                    copy_b(f, d, c, me).start()

        each_chunk(chunk)

    def permuted(f, k):
        return perm[f, pl.ds(k * repeat, repeat)].reshape(size, tokens)

    def back(t, l, k, value):
        f = step(t, l)
        rounded = (value * slope[f, k]).astype(BF16)
        scaled[f, k] = rounded
        work[work_rows(k), :] = dot_t(two[l, k], rounded)
        grad[k] = value
        product = value * silu[f, k]
        gate_acc[l, k] = product if t == 0 else gate_acc[l, k] + product

    def forward(t, l, then):
        f = step(t, l)

        def chunk(c):
            for d in (1, 2, 3):
                copy_f(f, d, c, partner(d)).wait_recv()
            for b in range(per):
                k = c * per + b
                mixed = dot(two[l, k], permuted(f, k))
                logistic = 0.5 + 0.5 * jnp.tanh(0.5 * mixed)
                branch = mixed * logistic
                scale = gate_b[l, k]
                if l + 1 < slots:
                    old = hidden(t, l)[k].astype(F32)
                    new = jnp.where(l < count, old + scale * branch, old).astype(BF16)
                    hid[t, l, k] = new
                    work[work_rows(k), :] = dot(one[l + 1, k], new)
                silu[f, k] = branch
                slope[f, k] = scale * (logistic * (1.0 + mixed * (1.0 - logistic)))
                if then is not None:
                    then(k)

        each_chunk(chunk)

    def backward(t, l, then):
        f = step(t, l)

        def chunk(c):
            for d in (1, 2, 3):
                copy_b(f, d, c, partner(d)).wait_recv()
            for b in range(per):
                k = c * per + b
                term = dot_t(one[l, k], ret[f, k].reshape(size, tokens))
                value = jnp.where(l < count, grad[k] + term, grad[k])
                then(k, value)
                if t == 1 and l == 0:
                    first_grad(0, k)
            if t == 0 and l == 0:
                hop_send(c)

        each_chunk(chunk)

    def hop_copy(c):
        part = pl.ds(c * per, per)
        return pltpu.make_async_remote_copy(
            src_ref=hop_out.at[part],
            dst_ref=hop_in.at[part],
            send_sem=hop_sent.at[c],
            recv_sem=hop_recv.at[c],
            device_id={"section": section - 1},
            device_id_type=MESH,
        )

    def hop_send(c):
        @pl.when(section > 0)
        def _():
            hop_copy(c).start()

    def second_grads(l):
        f, g = step(0, l), step(1, l)

        def block(k):
            left = jnp.concatenate([scaled[f, k], scaled[g, k]], axis=1)
            right = jnp.concatenate([permuted(f, k), permuted(g, k)], axis=1)
            total = lax.dot_general(left, right, (((1,), (1,)), ((), ())), preferred_element_type=F32)
            second_out[l, k] = jnp.where(l < count, total, 0.0).astype(BF16)
            gates = jnp.sum(gate_acc[l, k].T, axis=0, keepdims=True)
            gate_out[l, pl.ds(k, 1), :] = jnp.where(l < count, gates, 0.0)

        each_block(block)

    def first_grad(l, k):
            f, g = step(0, l), step(1, l)
            left = jnp.concatenate(
                [ret[f, k].reshape(size, tokens), ret[g, k].reshape(size, tokens)], axis=1
            )
            right = jnp.concatenate([hidden(0, l)[k], hidden(1, l)[k]], axis=1)
            total = lax.dot_general(left, right, (((1,), (1,)), ((), ())), preferred_element_type=F32)
            first_out[l, k] = jnp.where(l < count, total, 0.0).astype(BF16)

    def first_grads(l):
        each_block(functools.partial(first_grad, l))

    def start(t):
        def block(k):
            work[work_rows(k), :] = dot(one[0, k], inp[t, k])

        each_block(block)

    def widen(l):
        def block(k):
            gate_b[l, k] = jnp.broadcast_to(gate[l, pl.ds(k, 1), :], (size, size)).T

        each_block(block)

    load_inp(0).wait()
    load_one(0).wait()
    start(0)
    pl.semaphore_wait(
        barrier, 3 + jnp.where(section > 0, 1, 0) + jnp.where(section < last, 1, 0)
    )
    scatter_f(step(0, 0))
    load_inp(1).wait()
    start(1)
    scatter_f(step(1, 0))
    load_gate.wait()
    for l in range(slots):
        widen(l)
        load_two(l).wait()
        if l:
            load_one(l).wait()
    load_arr.wait()
    top = slots - 1
    for l in range(top):
        for t in (0, 1):
            forward(t, l, None)
            scatter_f(step(t, l + 1))
    forward(0, top, lambda k: back(0, top, k, arr[k].astype(F32)))
    scatter_b(step(0, top))
    forward(1, top, None)
    for l in range(top, 0, -1):
        backward(0, l, functools.partial(back, 0, l - 1))
        scatter_b(step(0, l - 1))

    def leave(k, value):
        hop_out[k] = value.astype(BF16)

    backward(0, 0, leave)

    @pl.when(section == last)
    def _():
        pltpu.make_async_copy(loss, hop_in, loss_sem).wait()

    def arrive(c):
        @pl.when(section < last)
        def _():
            hop_copy(c).wait_recv()

        for b in range(per):
            k = c * per + b
            back(1, top, k, hop_in[k].astype(F32))

    each_chunk(arrive)
    scatter_b(step(1, top))
    for l in range(top, 0, -1):
        second_grads(l)
        if l < top:
            first_grads(l + 1)
        backward(1, l, functools.partial(back, 1, l - 1))
        scatter_b(step(1, l - 1))
    second_grads(0)
    if top > 0:
        first_grads(1)

    def emit(k, value):
        emit_out[k] = value.astype(BF16)

    backward(1, 0, emit)

    for t in (0, 1):
        for l in range(slots):
            f = step(t, l)
            for d in (1, 2, 3):
                pltpu.make_async_remote_copy(
                    src_ref=send_f.at[f, d - 1], dst_ref=perm.at[f, :, me],
                    send_sem=sent_f.at[f, d - 1], recv_sem=recv_f.at[f, 0, d - 1],
                    device_id={"tensor": partner(d)}, device_id_type=MESH,
                ).wait_send()
                pltpu.make_async_remote_copy(
                    src_ref=send_b.at[f, d - 1], dst_ref=ret.at[f, :, me],
                    send_sem=sent_b.at[f, d - 1], recv_sem=recv_b.at[f, 0, d - 1],
                    device_id={"tensor": partner(d)}, device_id_type=MESH,
                ).wait_send()

    @pl.when(section > 0)
    def _():
        each_chunk(lambda c: hop_copy(c).wait_send())


def store_kernel(*refs):
    count = len(refs) // 2
    sems = refs[-1]
    copies = [
        pltpu.make_async_copy(refs[i], refs[count + i], sems.at[i]) for i in range(count)
    ]
    for copy in copies:
        copy.start()
    for copy in copies:
        copy.wait()


def store(values):
    return pl.pallas_call(
        store_kernel,
        out_shape=[jax.ShapeDtypeStruct(v.shape, v.dtype) for v in values],
        in_specs=[pl.BlockSpec(memory_space=pltpu.VMEM)] * len(values),
        out_specs=[pl.BlockSpec(memory_space=pl.ANY)] * len(values),
        scratch_shapes=[pltpu.SemaphoreType.DMA((len(values),))],
        compiler_params=pltpu.CompilerParams(vmem_limit_bytes=8 * 1024 * 1024),
    )(*values)


def fused_shards(
    section_inputs, arriving_grad, loss_grad, factor_first, factor_second, gate_scales, layer_count
):
    moments = section_inputs.shape[1]
    _, slots, blocks, size, _ = factor_first.shape
    tokens = section_inputs.shape[3]
    tensor = lax.axis_size("tensor")
    rows = size // tensor
    steps = moments * slots
    vmem = pl.BlockSpec(memory_space=pltpu.VMEM)
    block = (blocks, size, tokens)
    factor = (slots, blocks, size, size)
    outs = pl.pallas_call(
        kernel,
        out_shape=[
            pltpu.VMEM(block, BF16),
            pltpu.VMEM(factor, BF16),
            pltpu.VMEM(factor, BF16),
            pltpu.VMEM((slots, blocks, size), F32),
        ],
        in_specs=[pl.BlockSpec(memory_space=pl.ANY)] * 6 + [pl.BlockSpec(memory_space=pltpu.SMEM)],
        out_specs=[vmem] * 4,
        scratch_shapes=[
            pltpu.VMEM((moments,) + block, BF16),
            pltpu.VMEM(block, BF16),
            pltpu.VMEM(factor, BF16),
            pltpu.VMEM(factor, BF16),
            pltpu.VMEM((slots, blocks, size), F32),
            pltpu.VMEM((moments, max(slots - 1, 1)) + block, BF16),
            pltpu.VMEM((steps, rows, tensor, blocks, tokens), BF16),
            pltpu.VMEM((steps, blocks, tensor, rows, tokens), BF16),
            pltpu.VMEM((steps, 3, rows, blocks, tokens), BF16),
            pltpu.VMEM((steps, 3, blocks, rows, tokens), BF16),
            pltpu.VMEM((blocks * size, tokens), F32),
            pltpu.VMEM((steps,) + block, F32),
            pltpu.VMEM((steps,) + block, F32),
            pltpu.VMEM((slots,) + block, F32),
            pltpu.VMEM(block, F32),
            pltpu.VMEM((slots,) + block, F32),
            pltpu.VMEM((steps,) + block, BF16),
            pltpu.VMEM(block, BF16),
            pltpu.VMEM(block, BF16),
            pltpu.SemaphoreType.DMA((steps, CHUNKS, 3)),
            pltpu.SemaphoreType.DMA((steps, CHUNKS, 3)),
            pltpu.SemaphoreType.DMA((steps, 3)),
            pltpu.SemaphoreType.DMA((steps, 3)),
            pltpu.SemaphoreType.DMA((CHUNKS,)),
            pltpu.SemaphoreType.DMA((CHUNKS,)),
            pltpu.SemaphoreType.DMA(()),
            pltpu.SemaphoreType.DMA((moments,)),
            pltpu.SemaphoreType.DMA((slots,)),
            pltpu.SemaphoreType.DMA((slots,)),
            pltpu.SemaphoreType.DMA((2,)),
        ],
        compiler_params=pltpu.CompilerParams(
            collective_id=0, has_side_effects=True, vmem_limit_bytes=56 * 1024 * 1024
        ),
    )(
        section_inputs[0].reshape((moments,) + block),
        arriving_grad[0].reshape(block),
        loss_grad[0].reshape(block),
        factor_first[0],
        factor_second[0],
        gate_scales[0].reshape(slots, blocks, size),
        layer_count,
    )
    emitted, first_grad, second_grad, gate_grad = store(outs)
    return (
        emitted.reshape(1, blocks * size, tokens),
        first_grad[None],
        second_grad[None],
        gate_grad.reshape(1, slots, blocks * size),
    )


def solution(mesh):
    in_specs = (
        P("section", None, "tensor", None),
        P("section", "tensor", None),
        P(None, "tensor", None),
        P("section", None, "tensor", None, None),
        P("section", None, "tensor", None, None),
        P("section", None, "tensor"),
        P("section"),
    )
    out_specs = (
        P("section", "tensor", None),
        P("section", None, "tensor", None, None),
        P("section", None, "tensor", None, None),
        P("section", None, "tensor"),
    )
    fused = mesh.shape["tensor"] == 4
    return jax.shard_map(fused_shards if fused else shards, mesh=mesh, in_specs=in_specs, out_specs=out_specs, check_vma=False)
```

```python
import functools

import jax
import jax.numpy as jnp
from jax import lax
from jax.experimental import pallas as pl
from jax.experimental.pallas import tpu as pltpu
from jax.sharding import PartitionSpec as P


def from_behind(value, axis, steps):
    count = lax.axis_size(axis)
    initial, last = (max(0, -steps), min(count, count - steps))
    return lax.ppermute(value, axis, [(source, source + steps) for source in range(initial, last)])


def permute_blocks(values):
    tensor_size = lax.axis_size("tensor")
    batch_count, local_blocks, block_size, token_count = values.shape
    blocks_all = local_blocks * tensor_size
    repeat_count = block_size // blocks_all
    shaped = values.reshape(
        batch_count, local_blocks, tensor_size, local_blocks, repeat_count, token_count
    )
    moved = lax.all_to_all(shaped, "tensor", split_axis=2, concat_axis=1, tiled=True)
    moved = moved.reshape(batch_count, blocks_all, local_blocks, repeat_count, token_count)
    return moved.transpose(0, 2, 3, 1, 4).reshape(
        batch_count, local_blocks, block_size, token_count
    )


def unpermute_blocks(values):
    tensor_size = lax.axis_size("tensor")
    local_blocks, block_size, token_count = values.shape
    blocks_all = local_blocks * tensor_size
    repeat_count = block_size // blocks_all
    shaped = values.reshape(local_blocks, repeat_count, tensor_size, local_blocks, token_count)
    moved = lax.all_to_all(shaped, "tensor", split_axis=2, concat_axis=0, tiled=True)
    moved = moved.reshape(blocks_all, repeat_count, local_blocks, token_count)
    return moved.transpose(2, 0, 1, 3).reshape(local_blocks, block_size, token_count)


def recompute(initial, factor_one, factor_two, gate_rows, layer_total):
    slot_count = factor_one.shape[0]
    hidden = initial
    saved = []
    for layer_slot in range(slot_count):
        first_out = jnp.einsum(
            "kij,mkjt->mkit", factor_one[layer_slot], hidden, preferred_element_type=jnp.float32
        ).astype(jnp.bfloat16)
        permuted = permute_blocks(first_out)
        mixed = jnp.einsum(
            "kij,mkjt->mkit", factor_two[layer_slot], permuted, preferred_element_type=jnp.float32
        )
        gate_now = gate_rows[layer_slot][None, :, :, None]
        next_hidden = (
            hidden.astype(jnp.float32) + gate_now * (mixed * jax.nn.sigmoid(mixed))
        ).astype(jnp.bfloat16)
        saved.append((hidden, permuted, mixed))
        hidden = jnp.where(layer_slot < layer_total, next_hidden, hidden)
    return saved


def shards(
    section_inputs, arriving_grad, loss_grad, factor_first, factor_second, gate_scales, layer_count
):
    moments = section_inputs.shape[1]
    slot_count = factor_first.shape[1]
    local_blocks = factor_first.shape[2]
    block_size = factor_first.shape[3]
    token_count = section_inputs.shape[3]
    first_local = factor_first[0]
    second_local = factor_second[0]
    gate_rows = gate_scales[0].reshape(slot_count, local_blocks, block_size)
    layer_total = layer_count[0]
    section_id = lax.axis_index("section")
    last_section = lax.axis_size("section") - 1
    inputs_local = section_inputs[0].reshape(moments, local_blocks, block_size, token_count)
    first_acc = [
        jnp.zeros((local_blocks, block_size, block_size), jnp.float32) for slot in range(slot_count)
    ]
    second_acc = [
        jnp.zeros((local_blocks, block_size, block_size), jnp.float32) for slot in range(slot_count)
    ]
    gate_acc = [jnp.zeros((local_blocks, block_size), jnp.float32) for slot in range(slot_count)]
    emitted = None
    for moment in range(moments):
        if moment == 0:
            arrived = arriving_grad[0].reshape(local_blocks, block_size, token_count)
        else:
            shifted = from_behind(emitted, "section", -1)
            from_loss = loss_grad[moment - 1].reshape(local_blocks, block_size, token_count)
            arrived = jnp.where(section_id == last_section, from_loss, shifted)
        computed = recompute(
            inputs_local[moment : moment + 1], first_local, second_local, gate_rows, layer_total
        )
        saved = [(record[0][0], record[1][0], record[2][0]) for record in computed]
        grad_now = arrived.astype(jnp.float32)
        for layer_slot in reversed(range(slot_count)):
            hidden, permuted, mixed = saved[layer_slot]
            is_live = layer_slot < layer_total
            logistic = jax.nn.sigmoid(mixed)
            gate_now = gate_rows[layer_slot][:, :, None]
            gate_term = jnp.sum(grad_now * (mixed * logistic), axis=2)
            gate_acc[layer_slot] = gate_acc[layer_slot] + jnp.where(
                is_live, gate_term, jnp.zeros_like(gate_term)
            )
            scaled = (grad_now * gate_now * logistic * (1.0 + mixed * (1.0 - logistic))).astype(
                jnp.bfloat16
            )
            backed = jnp.einsum(
                "kji,kjt->kit", second_local[layer_slot], scaled, preferred_element_type=jnp.float32
            ).astype(jnp.bfloat16)
            returned = unpermute_blocks(backed)
            moved_grad = grad_now + jnp.einsum(
                "kji,kjt->kit",
                first_local[layer_slot],
                returned,
                preferred_element_type=jnp.float32,
            )
            grad_now = jnp.where(is_live, moved_grad, grad_now)
            second_term = jnp.einsum(
                "kit,kjt->kij", scaled, permuted, preferred_element_type=jnp.float32
            )
            first_term = jnp.einsum(
                "kit,kjt->kij", returned, hidden, preferred_element_type=jnp.float32
            )
            second_acc[layer_slot] = second_acc[layer_slot] + jnp.where(
                is_live, second_term, jnp.zeros_like(second_term)
            )
            first_acc[layer_slot] = first_acc[layer_slot] + jnp.where(
                is_live, first_term, jnp.zeros_like(first_term)
            )
        emitted = grad_now.astype(jnp.bfloat16)
    last_emitted = emitted.reshape(1, local_blocks * block_size, token_count)
    gate_out = jnp.stack(gate_acc).reshape(1, slot_count, local_blocks * block_size)
    first_out = jnp.stack(first_acc).astype(jnp.bfloat16)[None]
    second_out = jnp.stack(second_acc).astype(jnp.bfloat16)[None]
    return (last_emitted, first_out, second_out, gate_out)


MESH = pl.DeviceIdType.MESH
F32 = jnp.float32
BF16 = jnp.bfloat16
CHUNKS = 4


def kernel(
    inp_far, arr_far, loss, one_far, two_far, gate_far, count_ref,
    emit_out, first_out, second_out, gate_out,
    inp, arr, one, two, gate, hid, perm, ret, send_f, send_b, work, slope, silu, gate_b, grad, gate_acc, scaled,
    hop_in, hop_out,
    recv_f, recv_b, sent_f, sent_b, hop_recv, hop_sent, loss_sem,
    inp_sem, one_sem, two_sem, far_sem,
):
    slots, blocks, size, tokens = one.shape
    rows = perm.shape[1]
    repeat = rows // blocks
    per = blocks // CHUNKS
    span = rows // CHUNKS
    me = lax.axis_index("tensor")
    section = lax.axis_index("section")
    last = lax.axis_size("section") - 1
    me_low, me_high = me % 2, me // 2

    def partner(d):
        low = 1 - me_low if d % 2 else me_low
        high = 1 - me_high if d // 2 else me_high
        return high * 2 + low

    def load_inp(t):
        return pltpu.make_async_copy(inp_far.at[t], inp.at[t], inp_sem.at[t])

    def load_one(l):
        return pltpu.make_async_copy(one_far.at[l], one.at[l], one_sem.at[l])

    def load_two(l):
        return pltpu.make_async_copy(two_far.at[l], two.at[l], two_sem.at[l])

    load_gate = pltpu.make_async_copy(gate_far, gate, far_sem.at[0])
    load_arr = pltpu.make_async_copy(arr_far, arr, far_sem.at[1])
    load_inp(0).start()
    load_one(0).start()
    load_inp(1).start()
    load_gate.start()
    for l in range(slots):
        load_two(l).start()
        if l:
            load_one(l).start()
    load_arr.start()

    barrier = pltpu.get_barrier_semaphore()
    for d in (1, 2, 3):
        pl.semaphore_signal(
            barrier, inc=1, device_id={"tensor": partner(d)}, device_id_type=MESH
        )

    @pl.when(section > 0)
    def _():
        pl.semaphore_signal(barrier, inc=1, device_id={"section": section - 1}, device_id_type=MESH)

    @pl.when(section < last)
    def _():
        pl.semaphore_signal(barrier, inc=1, device_id={"section": section + 1}, device_id_type=MESH)

    @pl.when(section == last)
    def _():
        pltpu.make_async_copy(loss, hop_in, loss_sem).start()

    count = count_ref[0]

    def hidden(t, l):
        return inp.at[t] if l == 0 else hid.at[t, l - 1]

    def step(t, l):
        return t * slots + l

    def dot(a, b):
        return jnp.dot(a, b, preferred_element_type=F32)

    def dot_t(a, b):
        return lax.dot_general(a, b, (((0,), (0,)), ((), ())), preferred_element_type=F32)

    def work_rows(k):
        return pl.ds(pl.multiple_of(k * size, size), size)

    def each_chunk(body, low=0, high=CHUNKS):
        lax.fori_loop(low, high, lambda c, _: (body(c), 0)[1], 0)

    def room(t, l):
        return 0 if t == 0 else 1 + l % 2

    def beside(chunk, early, late):
        def body(c):
            if early is not None:
                pl.when(c == CHUNKS // 2)(early)
            if late is not None:
                pl.when(c == CHUNKS - 1)(late)
            chunk(c)

        each_chunk(body)

    def each_block(body):
        def chunk(c):
            for b in range(per):
                body(c * per + b)

        each_chunk(chunk)

    def copy_f(f, d, c, source):
        part = pl.ds(c * span, span)
        return pltpu.make_async_remote_copy(
            src_ref=send_f.at[f, d - 1, part],
            dst_ref=perm.at[f, part, source],
            send_sem=sent_f.at[f, d - 1],
            recv_sem=recv_f.at[f, c, d - 1],
            device_id={"tensor": partner(d)},
            device_id_type=MESH,
        )

    def copy_b(f, d, c, source):
        part = pl.ds(c * per, per)
        return pltpu.make_async_remote_copy(
            src_ref=send_b.at[f, d - 1, part],
            dst_ref=ret.at[f, part, source],
            send_sem=sent_b.at[f, d - 1],
            recv_sem=recv_b.at[f, c, d - 1],
            device_id={"tensor": partner(d)},
            device_id_type=MESH,
        )

    def scatter_f(t, l, low=0, high=CHUNKS):
        f = step(t, l)

        def chunk(c):
            for d in (3, 1, 2, 0):
                target = partner(d)
                for j in range(span):
                    row = c * span + j
                    tile = work[
                        room(t, l), pl.ds(target * rows + row, blocks, stride=size), :
                    ].astype(BF16)
                    if d:
                        send_f[f, d - 1, row] = tile
                    else:
                        perm[f, row, me] = tile
                if d:
                    copy_f(f, d, c, me).start()

        each_chunk(chunk, low, high)

    def scatter_b(f):
        def chunk(c):
            for d in (3, 1, 2, 0):
                target = partner(d)
                for j in range(per):
                    block = c * per + j
                    tile = work[
                        0, pl.ds(target * blocks + block, rows, stride=size // repeat), :
                    ].astype(BF16)
                    if d:
                        send_b[f, d - 1, block] = tile
                    else:
                        ret[f, block, me] = tile
                if d:
                    copy_b(f, d, c, me).start()

        each_chunk(chunk)

    def permuted(f, k):
        return perm[f, pl.ds(k * repeat, repeat)].reshape(size, tokens)

    def back(t, l, k, value):
        f = step(t, l)
        rounded = (value * slope[f, k]).astype(BF16)
        scaled[f, k] = rounded
        work[0, work_rows(k), :] = dot_t(two[l, k], rounded)
        grad[k] = value
        product = value * silu[f, k]
        gate_acc[l, k] = product if t == 0 else gate_acc[l, k] + product

    def forward(t, l, then, early=None, late=None, low=0, high=CHUNKS):
        f = step(t, l)

        def chunk(c):
            for d in (1, 2, 3):
                copy_f(f, d, c, partner(d)).wait_recv()
            for b in range(per):
                k = c * per + b
                mixed = dot(two[l, k], permuted(f, k))
                logistic = 0.5 + 0.5 * jnp.tanh(0.5 * mixed)
                branch = mixed * logistic
                scale = gate_b[l, k]
                if l + 1 < slots:
                    old = hidden(t, l)[k].astype(F32)
                    new = jnp.where(l < count, old + scale * branch, old).astype(BF16)
                    hid[t, l, k] = new
                    work[room(t, l + 1), work_rows(k), :] = dot(one[l + 1, k], new)
                silu[f, k] = branch
                slope[f, k] = scale * (logistic * (1.0 + mixed * (1.0 - logistic)))
                if then is not None:
                    then(k)

        if low or high < CHUNKS:
            each_chunk(chunk, low, high)
        else:
            beside(chunk, early, late)

    def backward(t, l, then, early=None, late=None):
        f = step(t, l)

        def chunk(c):
            for d in (1, 2, 3):
                copy_b(f, d, c, partner(d)).wait_recv()
            for b in range(per):
                k = c * per + b
                term = dot_t(one[l, k], ret[f, k].reshape(size, tokens))
                value = jnp.where(l < count, grad[k] + term, grad[k])
                then(k, value)
                if t == 1 and l == 0:
                    first_grad(0, k)
            if t == 0 and l == 0:
                hop_send(c)

        beside(chunk, early, late)

    def hop_copy(c):
        part = pl.ds(c * per, per)
        return pltpu.make_async_remote_copy(
            src_ref=hop_out.at[part],
            dst_ref=hop_in.at[part],
            send_sem=hop_sent.at[c],
            recv_sem=hop_recv.at[c],
            device_id={"section": section - 1},
            device_id_type=MESH,
        )

    def hop_send(c):
        @pl.when(section > 0)
        def _():
            hop_copy(c).start()

    def second_grads(l):
        f, g = step(0, l), step(1, l)

        def block(k):
            left = jnp.concatenate([scaled[f, k], scaled[g, k]], axis=1)
            right = jnp.concatenate([permuted(f, k), permuted(g, k)], axis=1)
            total = lax.dot_general(left, right, (((1,), (1,)), ((), ())), preferred_element_type=F32)
            second_out[l, k] = jnp.where(l < count, total, 0.0).astype(BF16)
            gates = jnp.sum(gate_acc[l, k].T, axis=0, keepdims=True)
            gate_out[l, pl.ds(k, 1), :] = jnp.where(l < count, gates, 0.0)

        each_block(block)

    def first_grad(l, k):
            f, g = step(0, l), step(1, l)
            left = jnp.concatenate(
                [ret[f, k].reshape(size, tokens), ret[g, k].reshape(size, tokens)], axis=1
            )
            right = jnp.concatenate([hidden(0, l)[k], hidden(1, l)[k]], axis=1)
            total = lax.dot_general(left, right, (((1,), (1,)), ((), ())), preferred_element_type=F32)
            first_out[l, k] = jnp.where(l < count, total, 0.0).astype(BF16)

    def first_grads(l):
        each_block(functools.partial(first_grad, l))

    def start(t):
        def block(k):
            work[room(t, 0), work_rows(k), :] = dot(one[0, k], inp[t, k])

        each_block(block)

    def widen(l):
        def block(k):
            gate_b[l, k] = jnp.broadcast_to(gate[l, pl.ds(k, 1), :], (size, size)).T

        each_block(block)

    load_inp(0).wait()
    load_one(0).wait()
    start(0)
    pl.semaphore_wait(
        barrier, 3 + jnp.where(section > 0, 1, 0) + jnp.where(section < last, 1, 0)
    )
    scatter_f(0, 0)
    load_inp(1).wait()
    start(1)
    load_gate.wait()
    widen(0)
    load_two(0).wait()

    half = CHUNKS // 2
    halves = [(0, half), (half, CHUNKS)]
    turns = [(l, h) for l in range(slots) for h in halves]

    def receive(n):
        if n <= 0 or n > len(turns):
            return None
        l, (low, high) = turns[n - 1]
        return lambda: forward(1, l, None, low=low, high=high)

    def send(n):
        if n >= len(turns):
            return None
        l, (low, high) = turns[n]
        return lambda: scatter_f(1, l, low, high)

    top = slots - 1
    turn = 0
    for l in range(top):
        load_one(l + 1).wait()
        forward(0, l, None, receive(turn), send(turn))
        turn += 1
        scatter_f(0, l + 1)
        widen(l + 1)
        load_two(l + 1).wait()
    load_arr.wait()
    forward(
        0, top, lambda k: back(0, top, k, arr[k].astype(F32)), receive(turn), send(turn)
    )
    turn += 1
    scatter_b(step(0, top))
    for l in range(top, 0, -1):
        backward(0, l, functools.partial(back, 0, l - 1), receive(turn), send(turn))
        turn += 1
        scatter_b(step(0, l - 1))

    def leave(k, value):
        hop_out[k] = value.astype(BF16)

    backward(0, 0, leave, receive(turn), send(turn))
    turn += 1

    @pl.when(section == last)
    def _():
        pltpu.make_async_copy(loss, hop_in, loss_sem).wait()

    def arrive(c):
        @pl.when(section < last)
        def _():
            hop_copy(c).wait_recv()

        for b in range(per):
            k = c * per + b
            back(1, top, k, hop_in[k].astype(F32))

    beside(arrive, receive(turn), None)
    scatter_b(step(1, top))
    for l in range(top, 0, -1):
        second_grads(l)
        if l < top:
            first_grads(l + 1)
        backward(1, l, functools.partial(back, 1, l - 1))
        scatter_b(step(1, l - 1))
    second_grads(0)
    if top > 0:
        first_grads(1)

    def emit(k, value):
        emit_out[k] = value.astype(BF16)

    backward(1, 0, emit)

    for t in (0, 1):
        for l in range(slots):
            f = step(t, l)
            for d in (1, 2, 3):
                pltpu.make_async_remote_copy(
                    src_ref=send_f.at[f, d - 1], dst_ref=perm.at[f, :, me],
                    send_sem=sent_f.at[f, d - 1], recv_sem=recv_f.at[f, 0, d - 1],
                    device_id={"tensor": partner(d)}, device_id_type=MESH,
                ).wait_send()
                pltpu.make_async_remote_copy(
                    src_ref=send_b.at[f, d - 1], dst_ref=ret.at[f, :, me],
                    send_sem=sent_b.at[f, d - 1], recv_sem=recv_b.at[f, 0, d - 1],
                    device_id={"tensor": partner(d)}, device_id_type=MESH,
                ).wait_send()

    @pl.when(section > 0)
    def _():
        each_chunk(lambda c: hop_copy(c).wait_send())


def store_kernel(*refs):
    count = len(refs) // 2
    sems = refs[-1]
    copies = [
        pltpu.make_async_copy(refs[i], refs[count + i], sems.at[i]) for i in range(count)
    ]
    for copy in copies:
        copy.start()
    for copy in copies:
        copy.wait()


def store(values):
    return pl.pallas_call(
        store_kernel,
        out_shape=[jax.ShapeDtypeStruct(v.shape, v.dtype) for v in values],
        in_specs=[pl.BlockSpec(memory_space=pltpu.VMEM)] * len(values),
        out_specs=[pl.BlockSpec(memory_space=pl.ANY)] * len(values),
        scratch_shapes=[pltpu.SemaphoreType.DMA((len(values),))],
        compiler_params=pltpu.CompilerParams(vmem_limit_bytes=8 * 1024 * 1024),
    )(*values)


def fused_shards(
    section_inputs, arriving_grad, loss_grad, factor_first, factor_second, gate_scales, layer_count
):
    moments = section_inputs.shape[1]
    _, slots, blocks, size, _ = factor_first.shape
    tokens = section_inputs.shape[3]
    tensor = lax.axis_size("tensor")
    rows = size // tensor
    steps = moments * slots
    vmem = pl.BlockSpec(memory_space=pltpu.VMEM)
    block = (blocks, size, tokens)
    factor = (slots, blocks, size, size)
    outs = pl.pallas_call(
        kernel,
        out_shape=[
            pltpu.VMEM(block, BF16),
            pltpu.VMEM(factor, BF16),
            pltpu.VMEM(factor, BF16),
            pltpu.VMEM((slots, blocks, size), F32),
        ],
        in_specs=[pl.BlockSpec(memory_space=pl.ANY)] * 6 + [pl.BlockSpec(memory_space=pltpu.SMEM)],
        out_specs=[vmem] * 4,
        scratch_shapes=[
            pltpu.VMEM((moments,) + block, BF16),
            pltpu.VMEM(block, BF16),
            pltpu.VMEM(factor, BF16),
            pltpu.VMEM(factor, BF16),
            pltpu.VMEM((slots, blocks, size), F32),
            pltpu.VMEM((moments, max(slots - 1, 1)) + block, BF16),
            pltpu.VMEM((steps, rows, tensor, blocks, tokens), BF16),
            pltpu.VMEM((steps, blocks, tensor, rows, tokens), BF16),
            pltpu.VMEM((steps, 3, rows, blocks, tokens), BF16),
            pltpu.VMEM((steps, 3, blocks, rows, tokens), BF16),
            pltpu.VMEM((3, blocks * size, tokens), F32),
            pltpu.VMEM((steps,) + block, F32),
            pltpu.VMEM((steps,) + block, F32),
            pltpu.VMEM((slots,) + block, F32),
            pltpu.VMEM(block, F32),
            pltpu.VMEM((slots,) + block, F32),
            pltpu.VMEM((steps,) + block, BF16),
            pltpu.VMEM(block, BF16),
            pltpu.VMEM(block, BF16),
            pltpu.SemaphoreType.DMA((steps, CHUNKS, 3)),
            pltpu.SemaphoreType.DMA((steps, CHUNKS, 3)),
            pltpu.SemaphoreType.DMA((steps, 3)),
            pltpu.SemaphoreType.DMA((steps, 3)),
            pltpu.SemaphoreType.DMA((CHUNKS,)),
            pltpu.SemaphoreType.DMA((CHUNKS,)),
            pltpu.SemaphoreType.DMA(()),
            pltpu.SemaphoreType.DMA((moments,)),
            pltpu.SemaphoreType.DMA((slots,)),
            pltpu.SemaphoreType.DMA((slots,)),
            pltpu.SemaphoreType.DMA((2,)),
        ],
        compiler_params=pltpu.CompilerParams(
            collective_id=0, has_side_effects=True, vmem_limit_bytes=56 * 1024 * 1024
        ),
    )(
        section_inputs[0].reshape((moments,) + block),
        arriving_grad[0].reshape(block),
        loss_grad[0].reshape(block),
        factor_first[0],
        factor_second[0],
        gate_scales[0].reshape(slots, blocks, size),
        layer_count,
    )
    emitted, first_grad, second_grad, gate_grad = store(outs)
    return (
        emitted.reshape(1, blocks * size, tokens),
        first_grad[None],
        second_grad[None],
        gate_grad.reshape(1, slots, blocks * size),
    )


def solution(mesh):
    in_specs = (
        P("section", None, "tensor", None),
        P("section", "tensor", None),
        P(None, "tensor", None),
        P("section", None, "tensor", None, None),
        P("section", None, "tensor", None, None),
        P("section", None, "tensor"),
        P("section"),
    )
    out_specs = (
        P("section", "tensor", None),
        P("section", None, "tensor", None, None),
        P("section", None, "tensor", None, None),
        P("section", None, "tensor"),
    )
    fused = mesh.shape["tensor"] == 4
    return jax.shard_map(fused_shards if fused else shards, mesh=mesh, in_specs=in_specs, out_specs=out_specs, check_vma=False)
```

```python
import functools

import jax
import jax.numpy as jnp
from jax import lax
from jax.experimental import pallas as pl
from jax.experimental.pallas import tpu as pltpu
from jax.sharding import PartitionSpec as P


def from_behind(value, axis, steps):
    count = lax.axis_size(axis)
    initial, last = (max(0, -steps), min(count, count - steps))
    return lax.ppermute(value, axis, [(source, source + steps) for source in range(initial, last)])


def permute_blocks(values):
    tensor_size = lax.axis_size("tensor")
    batch_count, local_blocks, block_size, token_count = values.shape
    blocks_all = local_blocks * tensor_size
    repeat_count = block_size // blocks_all
    shaped = values.reshape(
        batch_count, local_blocks, tensor_size, local_blocks, repeat_count, token_count
    )
    moved = lax.all_to_all(shaped, "tensor", split_axis=2, concat_axis=1, tiled=True)
    moved = moved.reshape(batch_count, blocks_all, local_blocks, repeat_count, token_count)
    return moved.transpose(0, 2, 3, 1, 4).reshape(
        batch_count, local_blocks, block_size, token_count
    )


def unpermute_blocks(values):
    tensor_size = lax.axis_size("tensor")
    local_blocks, block_size, token_count = values.shape
    blocks_all = local_blocks * tensor_size
    repeat_count = block_size // blocks_all
    shaped = values.reshape(local_blocks, repeat_count, tensor_size, local_blocks, token_count)
    moved = lax.all_to_all(shaped, "tensor", split_axis=2, concat_axis=0, tiled=True)
    moved = moved.reshape(blocks_all, repeat_count, local_blocks, token_count)
    return moved.transpose(2, 0, 1, 3).reshape(local_blocks, block_size, token_count)


def recompute(initial, factor_one, factor_two, gate_rows, layer_total):
    slot_count = factor_one.shape[0]
    hidden = initial
    saved = []
    for layer_slot in range(slot_count):
        first_out = jnp.einsum(
            "kij,mkjt->mkit", factor_one[layer_slot], hidden, preferred_element_type=jnp.float32
        ).astype(jnp.bfloat16)
        permuted = permute_blocks(first_out)
        mixed = jnp.einsum(
            "kij,mkjt->mkit", factor_two[layer_slot], permuted, preferred_element_type=jnp.float32
        )
        gate_now = gate_rows[layer_slot][None, :, :, None]
        next_hidden = (
            hidden.astype(jnp.float32) + gate_now * (mixed * jax.nn.sigmoid(mixed))
        ).astype(jnp.bfloat16)
        saved.append((hidden, permuted, mixed))
        hidden = jnp.where(layer_slot < layer_total, next_hidden, hidden)
    return saved


def shards(
    section_inputs, arriving_grad, loss_grad, factor_first, factor_second, gate_scales, layer_count
):
    moments = section_inputs.shape[1]
    slot_count = factor_first.shape[1]
    local_blocks = factor_first.shape[2]
    block_size = factor_first.shape[3]
    token_count = section_inputs.shape[3]
    first_local = factor_first[0]
    second_local = factor_second[0]
    gate_rows = gate_scales[0].reshape(slot_count, local_blocks, block_size)
    layer_total = layer_count[0]
    section_id = lax.axis_index("section")
    last_section = lax.axis_size("section") - 1
    inputs_local = section_inputs[0].reshape(moments, local_blocks, block_size, token_count)
    first_acc = [
        jnp.zeros((local_blocks, block_size, block_size), jnp.float32) for slot in range(slot_count)
    ]
    second_acc = [
        jnp.zeros((local_blocks, block_size, block_size), jnp.float32) for slot in range(slot_count)
    ]
    gate_acc = [jnp.zeros((local_blocks, block_size), jnp.float32) for slot in range(slot_count)]
    emitted = None
    for moment in range(moments):
        if moment == 0:
            arrived = arriving_grad[0].reshape(local_blocks, block_size, token_count)
        else:
            shifted = from_behind(emitted, "section", -1)
            from_loss = loss_grad[moment - 1].reshape(local_blocks, block_size, token_count)
            arrived = jnp.where(section_id == last_section, from_loss, shifted)
        computed = recompute(
            inputs_local[moment : moment + 1], first_local, second_local, gate_rows, layer_total
        )
        saved = [(record[0][0], record[1][0], record[2][0]) for record in computed]
        grad_now = arrived.astype(jnp.float32)
        for layer_slot in reversed(range(slot_count)):
            hidden, permuted, mixed = saved[layer_slot]
            is_live = layer_slot < layer_total
            logistic = jax.nn.sigmoid(mixed)
            gate_now = gate_rows[layer_slot][:, :, None]
            gate_term = jnp.sum(grad_now * (mixed * logistic), axis=2)
            gate_acc[layer_slot] = gate_acc[layer_slot] + jnp.where(
                is_live, gate_term, jnp.zeros_like(gate_term)
            )
            scaled = (grad_now * gate_now * logistic * (1.0 + mixed * (1.0 - logistic))).astype(
                jnp.bfloat16
            )
            backed = jnp.einsum(
                "kji,kjt->kit", second_local[layer_slot], scaled, preferred_element_type=jnp.float32
            ).astype(jnp.bfloat16)
            returned = unpermute_blocks(backed)
            moved_grad = grad_now + jnp.einsum(
                "kji,kjt->kit",
                first_local[layer_slot],
                returned,
                preferred_element_type=jnp.float32,
            )
            grad_now = jnp.where(is_live, moved_grad, grad_now)
            second_term = jnp.einsum(
                "kit,kjt->kij", scaled, permuted, preferred_element_type=jnp.float32
            )
            first_term = jnp.einsum(
                "kit,kjt->kij", returned, hidden, preferred_element_type=jnp.float32
            )
            second_acc[layer_slot] = second_acc[layer_slot] + jnp.where(
                is_live, second_term, jnp.zeros_like(second_term)
            )
            first_acc[layer_slot] = first_acc[layer_slot] + jnp.where(
                is_live, first_term, jnp.zeros_like(first_term)
            )
        emitted = grad_now.astype(jnp.bfloat16)
    last_emitted = emitted.reshape(1, local_blocks * block_size, token_count)
    gate_out = jnp.stack(gate_acc).reshape(1, slot_count, local_blocks * block_size)
    first_out = jnp.stack(first_acc).astype(jnp.bfloat16)[None]
    second_out = jnp.stack(second_acc).astype(jnp.bfloat16)[None]
    return (last_emitted, first_out, second_out, gate_out)


MESH = pl.DeviceIdType.MESH
F32 = jnp.float32
BF16 = jnp.bfloat16
CHUNKS = 4
AHEAD = 2


def kernel(
    inp_far, arr_far, loss, one_far, two_far, gate_far, count_ref,
    emit_out, first_out, second_out, gate_out,
    inp, arr, one, two, gate, hid, perm, ret, send_f, send_b, work, slope, silu, gate_b, grad, gate_acc, scaled,
    hop_in, hop_out,
    recv_f, recv_b, sent_f, sent_b, hop_recv, hop_sent, loss_sem,
    inp_sem, one_sem, two_sem, far_sem,
):
    slots, blocks, size, tokens = one.shape
    rows = perm.shape[1]
    repeat = rows // blocks
    per = blocks // CHUNKS
    span = rows // CHUNKS
    me = lax.axis_index("tensor")
    section = lax.axis_index("section")
    last = lax.axis_size("section") - 1
    me_low, me_high = me % 2, me // 2

    def partner(d):
        low = 1 - me_low if d % 2 else me_low
        high = 1 - me_high if d // 2 else me_high
        return high * 2 + low

    def load_inp(t):
        return pltpu.make_async_copy(inp_far.at[t], inp.at[t], inp_sem.at[t])

    def load_one(l):
        return pltpu.make_async_copy(one_far.at[l], one.at[l], one_sem.at[l])

    def load_two(l):
        return pltpu.make_async_copy(two_far.at[l], two.at[l], two_sem.at[l])

    load_gate = pltpu.make_async_copy(gate_far, gate, far_sem.at[0])
    load_arr = pltpu.make_async_copy(arr_far, arr, far_sem.at[1])
    load_inp(0).start()
    load_one(0).start()
    load_inp(1).start()
    load_gate.start()
    for l in range(slots):
        load_two(l).start()
        if l:
            load_one(l).start()
    load_arr.start()

    barrier = pltpu.get_barrier_semaphore()
    for d in (1, 2, 3):
        pl.semaphore_signal(
            barrier, inc=1, device_id={"tensor": partner(d)}, device_id_type=MESH
        )

    @pl.when(section > 0)
    def _():
        pl.semaphore_signal(barrier, inc=1, device_id={"section": section - 1}, device_id_type=MESH)

    @pl.when(section < last)
    def _():
        pl.semaphore_signal(barrier, inc=1, device_id={"section": section + 1}, device_id_type=MESH)

    @pl.when(section == last)
    def _():
        pltpu.make_async_copy(loss, hop_in, loss_sem).start()

    count = count_ref[0]

    def hidden(t, l):
        return inp.at[t] if l == 0 else hid.at[t, l - 1]

    def step(t, l):
        return t * slots + l

    def dot(a, b):
        return jnp.dot(a, b, preferred_element_type=F32)

    def dot_t(a, b):
        return lax.dot_general(a, b, (((0,), (0,)), ((), ())), preferred_element_type=F32)

    def work_rows(k):
        return pl.ds(pl.multiple_of(k * size, size), size)

    def each_chunk(body, low=0, high=CHUNKS):
        lax.fori_loop(low, high, lambda c, _: (body(c), 0)[1], 0)

    def room(t, l):
        return 0 if t == 0 else 1 + l % 2

    def beside(chunk, early, late):
        def body(c):
            if early is not None:
                pl.when(c == CHUNKS // 2)(early)
            if late is not None:
                pl.when(c == CHUNKS - 1)(late)
            chunk(c)

        each_chunk(body)

    def each_block(body):
        def chunk(c):
            for b in range(per):
                body(c * per + b)

        each_chunk(chunk)

    def copy_f(f, d, c, source):
        part = pl.ds(c * span, span)
        return pltpu.make_async_remote_copy(
            src_ref=send_f.at[f, d - 1, part],
            dst_ref=perm.at[f, part, source],
            send_sem=sent_f.at[f, d - 1],
            recv_sem=recv_f.at[f, c, d - 1],
            device_id={"tensor": partner(d)},
            device_id_type=MESH,
        )

    def copy_b(f, d, c, source):
        part = pl.ds(c * per, per)
        return pltpu.make_async_remote_copy(
            src_ref=send_b.at[f, d - 1, part],
            dst_ref=ret.at[f, part, source],
            send_sem=sent_b.at[f, d - 1],
            recv_sem=recv_b.at[f, c, d - 1],
            device_id={"tensor": partner(d)},
            device_id_type=MESH,
        )

    def scatter_f(t, l, low=0, high=CHUNKS):
        f = step(t, l)

        def chunk(c):
            for d in (3, 1, 2, 0):
                target = partner(d)
                for j in range(span):
                    row = c * span + j
                    tile = work[
                        room(t, l), pl.ds(target * rows + row, blocks, stride=size), :
                    ].astype(BF16)
                    if d:
                        send_f[f, d - 1, row] = tile
                    else:
                        perm[f, row, me] = tile
                if d and t:
                    copy_f(f, d, c, me).start()
                elif d:
                    pl.when(c < AHEAD)(copy_f(f, d, c, me).start)

        each_chunk(chunk, low, high)

    def scatter_b(f):
        def chunk(c):
            for d in (3, 1, 2, 0):
                target = partner(d)
                for j in range(per):
                    block = c * per + j
                    tile = work[
                        0, pl.ds(target * blocks + block, rows, stride=size // repeat), :
                    ].astype(BF16)
                    if d:
                        send_b[f, d - 1, block] = tile
                    else:
                        ret[f, block, me] = tile
                if d:
                    pl.when(c < AHEAD)(copy_b(f, d, c, me).start)

        each_chunk(chunk)

    def permuted(f, k):
        return perm[f, pl.ds(k * repeat, repeat)].reshape(size, tokens)

    def back(t, l, k, value):
        f = step(t, l)
        rounded = (value * slope[f, k]).astype(BF16)
        scaled[f, k] = rounded
        work[0, work_rows(k), :] = dot_t(two[l, k], rounded)
        grad[k] = value
        product = value * silu[f, k]
        gate_acc[l, k] = product if t == 0 else gate_acc[l, k] + product

    def forward(t, l, then, early=None, late=None, low=0, high=CHUNKS):
        f = step(t, l)

        def chunk(c):
            for d in (1, 2, 3):
                copy_f(f, d, c, partner(d)).wait_recv()
            if t == 0:
                for d in (3, 1, 2):
                    pl.when(c + AHEAD < CHUNKS)(copy_f(f, d, c + AHEAD, me).start)
            for b in range(per):
                k = c * per + b
                mixed = dot(two[l, k], permuted(f, k))
                logistic = 0.5 + 0.5 * jnp.tanh(0.5 * mixed)
                branch = mixed * logistic
                scale = gate_b[l, k]
                if l + 1 < slots:
                    old = hidden(t, l)[k].astype(F32)
                    new = jnp.where(l < count, old + scale * branch, old).astype(BF16)
                    hid[t, l, k] = new
                    work[room(t, l + 1), work_rows(k), :] = dot(one[l + 1, k], new)
                silu[f, k] = branch
                slope[f, k] = scale * (logistic * (1.0 + mixed * (1.0 - logistic)))
                if then is not None:
                    then(k)

        if low or high < CHUNKS:
            each_chunk(chunk, low, high)
        else:
            beside(chunk, early, late)

    def backward(t, l, then, early=None, late=None):
        f = step(t, l)

        def chunk(c):
            for d in (1, 2, 3):
                copy_b(f, d, c, partner(d)).wait_recv()
            for d in (3, 1, 2):
                pl.when(c + AHEAD < CHUNKS)(copy_b(f, d, c + AHEAD, me).start)
            for b in range(per):
                k = c * per + b
                term = dot_t(one[l, k], ret[f, k].reshape(size, tokens))
                value = jnp.where(l < count, grad[k] + term, grad[k])
                then(k, value)
                if t == 1 and l == 0:
                    first_grad(0, k)
            if t == 0 and l == 0:
                hop_send(c)

        beside(chunk, early, late)

    def hop_copy(c):
        part = pl.ds(c * per, per)
        return pltpu.make_async_remote_copy(
            src_ref=hop_out.at[part],
            dst_ref=hop_in.at[part],
            send_sem=hop_sent.at[c],
            recv_sem=hop_recv.at[c],
            device_id={"section": section - 1},
            device_id_type=MESH,
        )

    def hop_send(c):
        @pl.when(section > 0)
        def _():
            hop_copy(c).start()

    def second_grads(l):
        f, g = step(0, l), step(1, l)

        def block(k):
            left = jnp.concatenate([scaled[f, k], scaled[g, k]], axis=1)
            right = jnp.concatenate([permuted(f, k), permuted(g, k)], axis=1)
            total = lax.dot_general(left, right, (((1,), (1,)), ((), ())), preferred_element_type=F32)
            second_out[l, k] = jnp.where(l < count, total, 0.0).astype(BF16)
            gates = jnp.sum(gate_acc[l, k].T, axis=0, keepdims=True)
            gate_out[l, pl.ds(k, 1), :] = jnp.where(l < count, gates, 0.0)

        each_block(block)

    def first_grad(l, k):
            f, g = step(0, l), step(1, l)
            left = jnp.concatenate(
                [ret[f, k].reshape(size, tokens), ret[g, k].reshape(size, tokens)], axis=1
            )
            right = jnp.concatenate([hidden(0, l)[k], hidden(1, l)[k]], axis=1)
            total = lax.dot_general(left, right, (((1,), (1,)), ((), ())), preferred_element_type=F32)
            first_out[l, k] = jnp.where(l < count, total, 0.0).astype(BF16)

    def first_grads(l):
        each_block(functools.partial(first_grad, l))

    def start(t):
        def block(k):
            work[room(t, 0), work_rows(k), :] = dot(one[0, k], inp[t, k])

        each_block(block)

    def widen(l):
        def block(k):
            gate_b[l, k] = jnp.broadcast_to(gate[l, pl.ds(k, 1), :], (size, size)).T

        each_block(block)

    load_inp(0).wait()
    load_one(0).wait()
    start(0)
    pl.semaphore_wait(
        barrier, 3 + jnp.where(section > 0, 1, 0) + jnp.where(section < last, 1, 0)
    )
    scatter_f(0, 0)
    load_inp(1).wait()
    start(1)
    load_gate.wait()
    widen(0)
    load_two(0).wait()

    half = CHUNKS // 2
    halves = [(0, half), (half, CHUNKS)]
    turns = [(l, h) for l in range(slots) for h in halves]

    def receive(n):
        if n <= 0 or n > len(turns):
            return None
        l, (low, high) = turns[n - 1]
        return lambda: forward(1, l, None, low=low, high=high)

    def send(n):
        if n >= len(turns):
            return None
        l, (low, high) = turns[n]
        return lambda: scatter_f(1, l, low, high)

    top = slots - 1
    turn = 0
    for l in range(top):
        load_one(l + 1).wait()
        forward(0, l, None, receive(turn), send(turn))
        turn += 1
        scatter_f(0, l + 1)
        widen(l + 1)
        load_two(l + 1).wait()
    load_arr.wait()
    forward(
        0, top, lambda k: back(0, top, k, arr[k].astype(F32)), receive(turn), send(turn)
    )
    turn += 1
    scatter_b(step(0, top))
    for l in range(top, 0, -1):
        backward(0, l, functools.partial(back, 0, l - 1), receive(turn), send(turn))
        turn += 1
        scatter_b(step(0, l - 1))

    def leave(k, value):
        hop_out[k] = value.astype(BF16)

    backward(0, 0, leave, receive(turn), send(turn))
    turn += 1

    @pl.when(section == last)
    def _():
        pltpu.make_async_copy(loss, hop_in, loss_sem).wait()

    def arrive(c):
        @pl.when(section < last)
        def _():
            hop_copy(c).wait_recv()

        for b in range(per):
            k = c * per + b
            back(1, top, k, hop_in[k].astype(F32))

    beside(arrive, receive(turn), None)
    scatter_b(step(1, top))
    for l in range(top, 0, -1):
        second_grads(l)
        if l < top:
            first_grads(l + 1)
        backward(1, l, functools.partial(back, 1, l - 1))
        scatter_b(step(1, l - 1))
    second_grads(0)
    if top > 0:
        first_grads(1)

    def emit(k, value):
        emit_out[k] = value.astype(BF16)

    backward(1, 0, emit)

    for t in (0, 1):
        for l in range(slots):
            f = step(t, l)
            for d in (1, 2, 3):
                pltpu.make_async_remote_copy(
                    src_ref=send_f.at[f, d - 1], dst_ref=perm.at[f, :, me],
                    send_sem=sent_f.at[f, d - 1], recv_sem=recv_f.at[f, 0, d - 1],
                    device_id={"tensor": partner(d)}, device_id_type=MESH,
                ).wait_send()
                pltpu.make_async_remote_copy(
                    src_ref=send_b.at[f, d - 1], dst_ref=ret.at[f, :, me],
                    send_sem=sent_b.at[f, d - 1], recv_sem=recv_b.at[f, 0, d - 1],
                    device_id={"tensor": partner(d)}, device_id_type=MESH,
                ).wait_send()

    @pl.when(section > 0)
    def _():
        each_chunk(lambda c: hop_copy(c).wait_send())


def store_kernel(*refs):
    count = len(refs) // 2
    sems = refs[-1]
    copies = [
        pltpu.make_async_copy(refs[i], refs[count + i], sems.at[i]) for i in range(count)
    ]
    for copy in copies:
        copy.start()
    for copy in copies:
        copy.wait()


def store(values):
    return pl.pallas_call(
        store_kernel,
        out_shape=[jax.ShapeDtypeStruct(v.shape, v.dtype) for v in values],
        in_specs=[pl.BlockSpec(memory_space=pltpu.VMEM)] * len(values),
        out_specs=[pl.BlockSpec(memory_space=pl.ANY)] * len(values),
        scratch_shapes=[pltpu.SemaphoreType.DMA((len(values),))],
        compiler_params=pltpu.CompilerParams(vmem_limit_bytes=8 * 1024 * 1024),
    )(*values)


def fused_shards(
    section_inputs, arriving_grad, loss_grad, factor_first, factor_second, gate_scales, layer_count
):
    moments = section_inputs.shape[1]
    _, slots, blocks, size, _ = factor_first.shape
    tokens = section_inputs.shape[3]
    tensor = lax.axis_size("tensor")
    rows = size // tensor
    steps = moments * slots
    vmem = pl.BlockSpec(memory_space=pltpu.VMEM)
    block = (blocks, size, tokens)
    factor = (slots, blocks, size, size)
    outs = pl.pallas_call(
        kernel,
        out_shape=[
            pltpu.VMEM(block, BF16),
            pltpu.VMEM(factor, BF16),
            pltpu.VMEM(factor, BF16),
            pltpu.VMEM((slots, blocks, size), F32),
        ],
        in_specs=[pl.BlockSpec(memory_space=pl.ANY)] * 6 + [pl.BlockSpec(memory_space=pltpu.SMEM)],
        out_specs=[vmem] * 4,
        scratch_shapes=[
            pltpu.VMEM((moments,) + block, BF16),
            pltpu.VMEM(block, BF16),
            pltpu.VMEM(factor, BF16),
            pltpu.VMEM(factor, BF16),
            pltpu.VMEM((slots, blocks, size), F32),
            pltpu.VMEM((moments, max(slots - 1, 1)) + block, BF16),
            pltpu.VMEM((steps, rows, tensor, blocks, tokens), BF16),
            pltpu.VMEM((steps, blocks, tensor, rows, tokens), BF16),
            pltpu.VMEM((steps, 3, rows, blocks, tokens), BF16),
            pltpu.VMEM((steps, 3, blocks, rows, tokens), BF16),
            pltpu.VMEM((3, blocks * size, tokens), F32),
            pltpu.VMEM((steps,) + block, F32),
            pltpu.VMEM((steps,) + block, F32),
            pltpu.VMEM((slots,) + block, F32),
            pltpu.VMEM(block, F32),
            pltpu.VMEM((slots,) + block, F32),
            pltpu.VMEM((steps,) + block, BF16),
            pltpu.VMEM(block, BF16),
            pltpu.VMEM(block, BF16),
            pltpu.SemaphoreType.DMA((steps, CHUNKS, 3)),
            pltpu.SemaphoreType.DMA((steps, CHUNKS, 3)),
            pltpu.SemaphoreType.DMA((steps, 3)),
            pltpu.SemaphoreType.DMA((steps, 3)),
            pltpu.SemaphoreType.DMA((CHUNKS,)),
            pltpu.SemaphoreType.DMA((CHUNKS,)),
            pltpu.SemaphoreType.DMA(()),
            pltpu.SemaphoreType.DMA((moments,)),
            pltpu.SemaphoreType.DMA((slots,)),
            pltpu.SemaphoreType.DMA((slots,)),
            pltpu.SemaphoreType.DMA((2,)),
        ],
        compiler_params=pltpu.CompilerParams(
            collective_id=0, has_side_effects=True, vmem_limit_bytes=56 * 1024 * 1024
        ),
    )(
        section_inputs[0].reshape((moments,) + block),
        arriving_grad[0].reshape(block),
        loss_grad[0].reshape(block),
        factor_first[0],
        factor_second[0],
        gate_scales[0].reshape(slots, blocks, size),
        layer_count,
    )
    emitted, first_grad, second_grad, gate_grad = store(outs)
    return (
        emitted.reshape(1, blocks * size, tokens),
        first_grad[None],
        second_grad[None],
        gate_grad.reshape(1, slots, blocks * size),
    )


def solution(mesh):
    in_specs = (
        P("section", None, "tensor", None),
        P("section", "tensor", None),
        P(None, "tensor", None),
        P("section", None, "tensor", None, None),
        P("section", None, "tensor", None, None),
        P("section", None, "tensor"),
        P("section"),
    )
    out_specs = (
        P("section", "tensor", None),
        P("section", None, "tensor", None, None),
        P("section", None, "tensor", None, None),
        P("section", None, "tensor"),
    )
    fused = mesh.shape["tensor"] == 4
    return jax.shard_map(fused_shards if fused else shards, mesh=mesh, in_specs=in_specs, out_specs=out_specs, check_vma=False)
```

```python
import functools

import jax
import jax.numpy as jnp
from jax import lax
from jax.experimental import pallas as pl
from jax.experimental.pallas import tpu as pltpu
from jax.sharding import PartitionSpec as P


def from_behind(value, axis, steps):
    count = lax.axis_size(axis)
    initial, last = (max(0, -steps), min(count, count - steps))
    return lax.ppermute(value, axis, [(source, source + steps) for source in range(initial, last)])


def permute_blocks(values):
    tensor_size = lax.axis_size("tensor")
    batch_count, local_blocks, block_size, token_count = values.shape
    blocks_all = local_blocks * tensor_size
    repeat_count = block_size // blocks_all
    shaped = values.reshape(
        batch_count, local_blocks, tensor_size, local_blocks, repeat_count, token_count
    )
    moved = lax.all_to_all(shaped, "tensor", split_axis=2, concat_axis=1, tiled=True)
    moved = moved.reshape(batch_count, blocks_all, local_blocks, repeat_count, token_count)
    return moved.transpose(0, 2, 3, 1, 4).reshape(
        batch_count, local_blocks, block_size, token_count
    )


def unpermute_blocks(values):
    tensor_size = lax.axis_size("tensor")
    local_blocks, block_size, token_count = values.shape
    blocks_all = local_blocks * tensor_size
    repeat_count = block_size // blocks_all
    shaped = values.reshape(local_blocks, repeat_count, tensor_size, local_blocks, token_count)
    moved = lax.all_to_all(shaped, "tensor", split_axis=2, concat_axis=0, tiled=True)
    moved = moved.reshape(blocks_all, repeat_count, local_blocks, token_count)
    return moved.transpose(2, 0, 1, 3).reshape(local_blocks, block_size, token_count)


def recompute(initial, factor_one, factor_two, gate_rows, layer_total):
    slot_count = factor_one.shape[0]
    hidden = initial
    saved = []
    for layer_slot in range(slot_count):
        first_out = jnp.einsum(
            "kij,mkjt->mkit", factor_one[layer_slot], hidden, preferred_element_type=jnp.float32
        ).astype(jnp.bfloat16)
        permuted = permute_blocks(first_out)
        mixed = jnp.einsum(
            "kij,mkjt->mkit", factor_two[layer_slot], permuted, preferred_element_type=jnp.float32
        )
        gate_now = gate_rows[layer_slot][None, :, :, None]
        next_hidden = (
            hidden.astype(jnp.float32) + gate_now * (mixed * jax.nn.sigmoid(mixed))
        ).astype(jnp.bfloat16)
        saved.append((hidden, permuted, mixed))
        hidden = jnp.where(layer_slot < layer_total, next_hidden, hidden)
    return saved


def shards(
    section_inputs, arriving_grad, loss_grad, factor_first, factor_second, gate_scales, layer_count
):
    moments = section_inputs.shape[1]
    slot_count = factor_first.shape[1]
    local_blocks = factor_first.shape[2]
    block_size = factor_first.shape[3]
    token_count = section_inputs.shape[3]
    first_local = factor_first[0]
    second_local = factor_second[0]
    gate_rows = gate_scales[0].reshape(slot_count, local_blocks, block_size)
    layer_total = layer_count[0]
    section_id = lax.axis_index("section")
    last_section = lax.axis_size("section") - 1
    inputs_local = section_inputs[0].reshape(moments, local_blocks, block_size, token_count)
    first_acc = [
        jnp.zeros((local_blocks, block_size, block_size), jnp.float32) for slot in range(slot_count)
    ]
    second_acc = [
        jnp.zeros((local_blocks, block_size, block_size), jnp.float32) for slot in range(slot_count)
    ]
    gate_acc = [jnp.zeros((local_blocks, block_size), jnp.float32) for slot in range(slot_count)]
    emitted = None
    for moment in range(moments):
        if moment == 0:
            arrived = arriving_grad[0].reshape(local_blocks, block_size, token_count)
        else:
            shifted = from_behind(emitted, "section", -1)
            from_loss = loss_grad[moment - 1].reshape(local_blocks, block_size, token_count)
            arrived = jnp.where(section_id == last_section, from_loss, shifted)
        computed = recompute(
            inputs_local[moment : moment + 1], first_local, second_local, gate_rows, layer_total
        )
        saved = [(record[0][0], record[1][0], record[2][0]) for record in computed]
        grad_now = arrived.astype(jnp.float32)
        for layer_slot in reversed(range(slot_count)):
            hidden, permuted, mixed = saved[layer_slot]
            is_live = layer_slot < layer_total
            logistic = jax.nn.sigmoid(mixed)
            gate_now = gate_rows[layer_slot][:, :, None]
            gate_term = jnp.sum(grad_now * (mixed * logistic), axis=2)
            gate_acc[layer_slot] = gate_acc[layer_slot] + jnp.where(
                is_live, gate_term, jnp.zeros_like(gate_term)
            )
            scaled = (grad_now * gate_now * logistic * (1.0 + mixed * (1.0 - logistic))).astype(
                jnp.bfloat16
            )
            backed = jnp.einsum(
                "kji,kjt->kit", second_local[layer_slot], scaled, preferred_element_type=jnp.float32
            ).astype(jnp.bfloat16)
            returned = unpermute_blocks(backed)
            moved_grad = grad_now + jnp.einsum(
                "kji,kjt->kit",
                first_local[layer_slot],
                returned,
                preferred_element_type=jnp.float32,
            )
            grad_now = jnp.where(is_live, moved_grad, grad_now)
            second_term = jnp.einsum(
                "kit,kjt->kij", scaled, permuted, preferred_element_type=jnp.float32
            )
            first_term = jnp.einsum(
                "kit,kjt->kij", returned, hidden, preferred_element_type=jnp.float32
            )
            second_acc[layer_slot] = second_acc[layer_slot] + jnp.where(
                is_live, second_term, jnp.zeros_like(second_term)
            )
            first_acc[layer_slot] = first_acc[layer_slot] + jnp.where(
                is_live, first_term, jnp.zeros_like(first_term)
            )
        emitted = grad_now.astype(jnp.bfloat16)
    last_emitted = emitted.reshape(1, local_blocks * block_size, token_count)
    gate_out = jnp.stack(gate_acc).reshape(1, slot_count, local_blocks * block_size)
    first_out = jnp.stack(first_acc).astype(jnp.bfloat16)[None]
    second_out = jnp.stack(second_acc).astype(jnp.bfloat16)[None]
    return (last_emitted, first_out, second_out, gate_out)


MESH = pl.DeviceIdType.MESH
F32 = jnp.float32
BF16 = jnp.bfloat16
CHUNKS = 4


def kernel(
    inp_far, arr_far, loss, one_far, two_far, gate_far, count_ref,
    emit_out, first_out, second_out, gate_out,
    inp, arr, one, two, one_t, two_t, gate, hid, perm, ret, send_f, send_b, work, slope, silu, gate_b, grad, gate_acc, scaled,
    hop_in, hop_out,
    recv_f, recv_b, sent_f, sent_b, hop_recv, hop_sent, loss_sem,
    inp_sem, one_sem, two_sem, far_sem,
):
    slots, blocks, size, tokens = one.shape
    rows = perm.shape[1]
    repeat = rows // blocks
    per = blocks // CHUNKS
    span = rows // CHUNKS
    me = lax.axis_index("tensor")
    section = lax.axis_index("section")
    last = lax.axis_size("section") - 1
    me_low, me_high = me % 2, me // 2

    def partner(d):
        low = 1 - me_low if d % 2 else me_low
        high = 1 - me_high if d // 2 else me_high
        return high * 2 + low

    def load_inp(t):
        return pltpu.make_async_copy(inp_far.at[t], inp.at[t], inp_sem.at[t])

    def load_one(l):
        return pltpu.make_async_copy(one_far.at[l], one.at[l], one_sem.at[l])

    def load_two(l):
        return pltpu.make_async_copy(two_far.at[l], two.at[l], two_sem.at[l])

    load_gate = pltpu.make_async_copy(gate_far, gate, far_sem.at[0])
    load_arr = pltpu.make_async_copy(arr_far, arr, far_sem.at[1])
    load_inp(0).start()
    load_one(0).start()
    load_inp(1).start()
    load_gate.start()
    for l in range(slots):
        load_two(l).start()
        if l:
            load_one(l).start()
    load_arr.start()

    barrier = pltpu.get_barrier_semaphore()
    for d in (1, 2, 3):
        pl.semaphore_signal(
            barrier, inc=1, device_id={"tensor": partner(d)}, device_id_type=MESH
        )

    @pl.when(section > 0)
    def _():
        pl.semaphore_signal(barrier, inc=1, device_id={"section": section - 1}, device_id_type=MESH)

    @pl.when(section < last)
    def _():
        pl.semaphore_signal(barrier, inc=1, device_id={"section": section + 1}, device_id_type=MESH)

    @pl.when(section == last)
    def _():
        pltpu.make_async_copy(loss, hop_in, loss_sem).start()

    count = count_ref[0]

    def hidden(t, l):
        return inp.at[t] if l == 0 else hid.at[t, l - 1]

    def step(t, l):
        return t * slots + l

    def dot(a, b):
        return jnp.dot(a, b, preferred_element_type=F32)


    def work_rows(k):
        return pl.ds(pl.multiple_of(k * size, size), size)

    def each_chunk(body, low=0, high=CHUNKS):
        lax.fori_loop(low, high, lambda c, _: (body(c), 0)[1], 0)

    def room(t, l):
        return 0 if t == 0 else 1 + l % 2

    def beside(chunk, early, late):
        def body(c):
            if early is not None:
                pl.when(c == CHUNKS // 2)(early)
            if late is not None:
                pl.when(c == CHUNKS - 1)(late)
            chunk(c)

        each_chunk(body)

    def each_block(body):
        def chunk(c):
            for b in range(per):
                body(c * per + b)

        each_chunk(chunk)

    def copy_f(f, d, c, source):
        part = pl.ds(c * span, span)
        return pltpu.make_async_remote_copy(
            src_ref=send_f.at[f, d - 1, part],
            dst_ref=perm.at[f, part, source],
            send_sem=sent_f.at[f, d - 1],
            recv_sem=recv_f.at[f, c, d - 1],
            device_id={"tensor": partner(d)},
            device_id_type=MESH,
        )

    def copy_b(f, d, c, source):
        part = pl.ds(c * per, per)
        return pltpu.make_async_remote_copy(
            src_ref=send_b.at[f, d - 1, part],
            dst_ref=ret.at[f, part, source],
            send_sem=sent_b.at[f, d - 1],
            recv_sem=recv_b.at[f, c, d - 1],
            device_id={"tensor": partner(d)},
            device_id_type=MESH,
        )

    def scatter_f(t, l, low=0, high=CHUNKS):
        f = step(t, l)

        def chunk(c):
            for d in (3, 1, 2, 0):
                target = partner(d)
                for j in range(span):
                    row = c * span + j
                    tile = work[
                        room(t, l), pl.ds(target * rows + row, blocks, stride=size), :
                    ].astype(BF16)
                    if d:
                        send_f[f, d - 1, row] = tile
                    else:
                        perm[f, row, me] = tile
                if d:
                    copy_f(f, d, c, me).start()

        each_chunk(chunk, low, high)

    def scatter_b(f):
        def chunk(c):
            for d in (3, 1, 2, 0):
                target = partner(d)
                for j in range(per):
                    block = c * per + j
                    tile = work[
                        0, pl.ds(target * blocks + block, rows, stride=size // repeat), :
                    ].astype(BF16)
                    if d:
                        send_b[f, d - 1, block] = tile
                    else:
                        ret[f, block, me] = tile
                if d:
                    copy_b(f, d, c, me).start()

        each_chunk(chunk)

    def permuted(f, k):
        return perm[f, pl.ds(k * repeat, repeat)].reshape(size, tokens)

    def back(t, l, k, value):
        f = step(t, l)
        rounded = (value * slope[f, k]).astype(BF16)
        scaled[f, k] = rounded
        work[0, work_rows(k), :] = dot(two_t[l, k], rounded)
        grad[k] = value
        product = value * silu[f, k]
        gate_acc[l, k] = product if t == 0 else gate_acc[l, k] + product

    def forward(t, l, then, early=None, late=None, low=0, high=CHUNKS):
        f = step(t, l)

        def chunk(c):
            for d in (1, 2, 3):
                copy_f(f, d, c, partner(d)).wait_recv()
            for b in range(per):
                k = c * per + b
                mixed = dot(two[l, k], permuted(f, k))
                logistic = 0.5 + 0.5 * jnp.tanh(0.5 * mixed)
                branch = mixed * logistic
                scale = gate_b[l, k]
                if l + 1 < slots:
                    old = hidden(t, l)[k].astype(F32)
                    new = jnp.where(l < count, old + scale * branch, old).astype(BF16)
                    hid[t, l, k] = new
                    work[room(t, l + 1), work_rows(k), :] = dot(one[l + 1, k], new)
                silu[f, k] = branch
                slope[f, k] = scale * (logistic * (1.0 + mixed * (1.0 - logistic)))
                if then is not None:
                    then(k)

        if low or high < CHUNKS:
            each_chunk(chunk, low, high)
        else:
            beside(chunk, early, late)

    def backward(t, l, then, early=None, late=None):
        f = step(t, l)

        def chunk(c):
            for d in (1, 2, 3):
                copy_b(f, d, c, partner(d)).wait_recv()
            for b in range(per):
                k = c * per + b
                term = dot(one_t[l, k], ret[f, k].reshape(size, tokens))
                value = jnp.where(l < count, grad[k] + term, grad[k])
                then(k, value)
                if t == 1 and l == 0:
                    first_grad(0, k)
            if t == 0 and l == 0:
                hop_send(c)

        beside(chunk, early, late)

    def hop_copy(c):
        part = pl.ds(c * per, per)
        return pltpu.make_async_remote_copy(
            src_ref=hop_out.at[part],
            dst_ref=hop_in.at[part],
            send_sem=hop_sent.at[c],
            recv_sem=hop_recv.at[c],
            device_id={"section": section - 1},
            device_id_type=MESH,
        )

    def hop_send(c):
        @pl.when(section > 0)
        def _():
            hop_copy(c).start()

    def second_grads(l):
        f, g = step(0, l), step(1, l)

        def block(k):
            left = jnp.concatenate([scaled[f, k], scaled[g, k]], axis=1)
            right = jnp.concatenate([permuted(f, k), permuted(g, k)], axis=1)
            total = lax.dot_general(left, right, (((1,), (1,)), ((), ())), preferred_element_type=F32)
            second_out[l, k] = jnp.where(l < count, total, 0.0).astype(BF16)
            gates = jnp.sum(gate_acc[l, k].T, axis=0, keepdims=True)
            gate_out[l, pl.ds(k, 1), :] = jnp.where(l < count, gates, 0.0)

        each_block(block)

    def first_grad(l, k):
            f, g = step(0, l), step(1, l)
            left = jnp.concatenate(
                [ret[f, k].reshape(size, tokens), ret[g, k].reshape(size, tokens)], axis=1
            )
            right = jnp.concatenate([hidden(0, l)[k], hidden(1, l)[k]], axis=1)
            total = lax.dot_general(left, right, (((1,), (1,)), ((), ())), preferred_element_type=F32)
            first_out[l, k] = jnp.where(l < count, total, 0.0).astype(BF16)

    def first_grads(l):
        each_block(functools.partial(first_grad, l))

    def start(t):
        def block(k):
            work[room(t, 0), work_rows(k), :] = dot(one[0, k], inp[t, k])

        each_block(block)

    def widen(l):
        def block(k):
            gate_b[l, k] = jnp.broadcast_to(gate[l, pl.ds(k, 1), :], (size, size)).T

        each_block(block)

    def turn_over(source, target, l):
        def block(k):
            target[l, k] = source[l, k].T

        each_block(block)

    load_inp(0).wait()
    load_one(0).wait()
    start(0)
    pl.semaphore_wait(
        barrier, 3 + jnp.where(section > 0, 1, 0) + jnp.where(section < last, 1, 0)
    )
    scatter_f(0, 0)
    load_inp(1).wait()
    start(1)
    load_gate.wait()
    widen(0)
    load_two(0).wait()

    half = CHUNKS // 2
    halves = [(0, half), (half, CHUNKS)]
    turns = [(l, h) for l in range(slots) for h in halves]

    def receive(n):
        if n <= 0 or n > len(turns):
            return None
        l, (low, high) = turns[n - 1]
        return lambda: forward(1, l, None, low=low, high=high)

    def send(n):
        if n >= len(turns):
            return None
        l, (low, high) = turns[n]
        return lambda: scatter_f(1, l, low, high)

    top = slots - 1
    turn = 0
    for l in range(top):
        load_one(l + 1).wait()
        forward(0, l, None, receive(turn), send(turn))
        turn += 1
        scatter_f(0, l + 1)
        widen(l + 1)
        load_two(l + 1).wait()
    load_arr.wait()
    turn_over(two, two_t, top)
    forward(
        0, top, lambda k: back(0, top, k, arr[k].astype(F32)), receive(turn), send(turn)
    )
    turn += 1
    scatter_b(step(0, top))
    for l in range(top, 0, -1):
        turn_over(one, one_t, l)
        turn_over(two, two_t, l - 1)
        backward(0, l, functools.partial(back, 0, l - 1), receive(turn), send(turn))
        turn += 1
        scatter_b(step(0, l - 1))

    def leave(k, value):
        hop_out[k] = value.astype(BF16)

    turn_over(one, one_t, 0)
    backward(0, 0, leave, receive(turn), send(turn))
    turn += 1

    @pl.when(section == last)
    def _():
        pltpu.make_async_copy(loss, hop_in, loss_sem).wait()

    def arrive(c):
        @pl.when(section < last)
        def _():
            hop_copy(c).wait_recv()

        for b in range(per):
            k = c * per + b
            back(1, top, k, hop_in[k].astype(F32))

    beside(arrive, receive(turn), None)
    scatter_b(step(1, top))
    for l in range(top, 0, -1):
        second_grads(l)
        if l < top:
            first_grads(l + 1)
        backward(1, l, functools.partial(back, 1, l - 1))
        scatter_b(step(1, l - 1))
    second_grads(0)
    if top > 0:
        first_grads(1)

    def emit(k, value):
        emit_out[k] = value.astype(BF16)

    backward(1, 0, emit)

    for t in (0, 1):
        for l in range(slots):
            f = step(t, l)
            for d in (1, 2, 3):
                pltpu.make_async_remote_copy(
                    src_ref=send_f.at[f, d - 1], dst_ref=perm.at[f, :, me],
                    send_sem=sent_f.at[f, d - 1], recv_sem=recv_f.at[f, 0, d - 1],
                    device_id={"tensor": partner(d)}, device_id_type=MESH,
                ).wait_send()
                pltpu.make_async_remote_copy(
                    src_ref=send_b.at[f, d - 1], dst_ref=ret.at[f, :, me],
                    send_sem=sent_b.at[f, d - 1], recv_sem=recv_b.at[f, 0, d - 1],
                    device_id={"tensor": partner(d)}, device_id_type=MESH,
                ).wait_send()

    @pl.when(section > 0)
    def _():
        each_chunk(lambda c: hop_copy(c).wait_send())


def store_kernel(*refs):
    count = len(refs) // 2
    sems = refs[-1]
    copies = [
        pltpu.make_async_copy(refs[i], refs[count + i], sems.at[i]) for i in range(count)
    ]
    for copy in copies:
        copy.start()
    for copy in copies:
        copy.wait()


def store(values):
    return pl.pallas_call(
        store_kernel,
        out_shape=[jax.ShapeDtypeStruct(v.shape, v.dtype) for v in values],
        in_specs=[pl.BlockSpec(memory_space=pltpu.VMEM)] * len(values),
        out_specs=[pl.BlockSpec(memory_space=pl.ANY)] * len(values),
        scratch_shapes=[pltpu.SemaphoreType.DMA((len(values),))],
        compiler_params=pltpu.CompilerParams(vmem_limit_bytes=8 * 1024 * 1024),
    )(*values)


def fused_shards(
    section_inputs, arriving_grad, loss_grad, factor_first, factor_second, gate_scales, layer_count
):
    moments = section_inputs.shape[1]
    _, slots, blocks, size, _ = factor_first.shape
    tokens = section_inputs.shape[3]
    tensor = lax.axis_size("tensor")
    rows = size // tensor
    steps = moments * slots
    vmem = pl.BlockSpec(memory_space=pltpu.VMEM)
    block = (blocks, size, tokens)
    factor = (slots, blocks, size, size)
    outs = pl.pallas_call(
        kernel,
        out_shape=[
            pltpu.VMEM(block, BF16),
            pltpu.VMEM(factor, BF16),
            pltpu.VMEM(factor, BF16),
            pltpu.VMEM((slots, blocks, size), F32),
        ],
        in_specs=[pl.BlockSpec(memory_space=pl.ANY)] * 6 + [pl.BlockSpec(memory_space=pltpu.SMEM)],
        out_specs=[vmem] * 4,
        scratch_shapes=[
            pltpu.VMEM((moments,) + block, BF16),
            pltpu.VMEM(block, BF16),
            pltpu.VMEM(factor, BF16),
            pltpu.VMEM(factor, BF16),
            pltpu.VMEM(factor, BF16),
            pltpu.VMEM(factor, BF16),
            pltpu.VMEM((slots, blocks, size), F32),
            pltpu.VMEM((moments, max(slots - 1, 1)) + block, BF16),
            pltpu.VMEM((steps, rows, tensor, blocks, tokens), BF16),
            pltpu.VMEM((steps, blocks, tensor, rows, tokens), BF16),
            pltpu.VMEM((steps, 3, rows, blocks, tokens), BF16),
            pltpu.VMEM((steps, 3, blocks, rows, tokens), BF16),
            pltpu.VMEM((3, blocks * size, tokens), F32),
            pltpu.VMEM((steps,) + block, F32),
            pltpu.VMEM((steps,) + block, F32),
            pltpu.VMEM((slots,) + block, F32),
            pltpu.VMEM(block, F32),
            pltpu.VMEM((slots,) + block, F32),
            pltpu.VMEM((steps,) + block, BF16),
            pltpu.VMEM(block, BF16),
            pltpu.VMEM(block, BF16),
            pltpu.SemaphoreType.DMA((steps, CHUNKS, 3)),
            pltpu.SemaphoreType.DMA((steps, CHUNKS, 3)),
            pltpu.SemaphoreType.DMA((steps, 3)),
            pltpu.SemaphoreType.DMA((steps, 3)),
            pltpu.SemaphoreType.DMA((CHUNKS,)),
            pltpu.SemaphoreType.DMA((CHUNKS,)),
            pltpu.SemaphoreType.DMA(()),
            pltpu.SemaphoreType.DMA((moments,)),
            pltpu.SemaphoreType.DMA((slots,)),
            pltpu.SemaphoreType.DMA((slots,)),
            pltpu.SemaphoreType.DMA((2,)),
        ],
        compiler_params=pltpu.CompilerParams(
            collective_id=0, has_side_effects=True, vmem_limit_bytes=56 * 1024 * 1024
        ),
    )(
        section_inputs[0].reshape((moments,) + block),
        arriving_grad[0].reshape(block),
        loss_grad[0].reshape(block),
        factor_first[0],
        factor_second[0],
        gate_scales[0].reshape(slots, blocks, size),
        layer_count,
    )
    emitted, first_grad, second_grad, gate_grad = store(outs)
    return (
        emitted.reshape(1, blocks * size, tokens),
        first_grad[None],
        second_grad[None],
        gate_grad.reshape(1, slots, blocks * size),
    )


def solution(mesh):
    in_specs = (
        P("section", None, "tensor", None),
        P("section", "tensor", None),
        P(None, "tensor", None),
        P("section", None, "tensor", None, None),
        P("section", None, "tensor", None, None),
        P("section", None, "tensor"),
        P("section"),
    )
    out_specs = (
        P("section", "tensor", None),
        P("section", None, "tensor", None, None),
        P("section", None, "tensor", None, None),
        P("section", None, "tensor"),
    )
    fused = mesh.shape["tensor"] == 4
    return jax.shard_map(fused_shards if fused else shards, mesh=mesh, in_specs=in_specs, out_specs=out_specs, check_vma=False)
```

```python
import functools

import jax
import jax.numpy as jnp
from jax import lax
from jax.experimental import pallas as pl
from jax.experimental.pallas import tpu as pltpu
from jax.sharding import PartitionSpec as P


def from_behind(value, axis, steps):
    count = lax.axis_size(axis)
    initial, last = (max(0, -steps), min(count, count - steps))
    return lax.ppermute(value, axis, [(source, source + steps) for source in range(initial, last)])


def permute_blocks(values):
    tensor_size = lax.axis_size("tensor")
    batch_count, local_blocks, block_size, token_count = values.shape
    blocks_all = local_blocks * tensor_size
    repeat_count = block_size // blocks_all
    shaped = values.reshape(
        batch_count, local_blocks, tensor_size, local_blocks, repeat_count, token_count
    )
    moved = lax.all_to_all(shaped, "tensor", split_axis=2, concat_axis=1, tiled=True)
    moved = moved.reshape(batch_count, blocks_all, local_blocks, repeat_count, token_count)
    return moved.transpose(0, 2, 3, 1, 4).reshape(
        batch_count, local_blocks, block_size, token_count
    )


def unpermute_blocks(values):
    tensor_size = lax.axis_size("tensor")
    local_blocks, block_size, token_count = values.shape
    blocks_all = local_blocks * tensor_size
    repeat_count = block_size // blocks_all
    shaped = values.reshape(local_blocks, repeat_count, tensor_size, local_blocks, token_count)
    moved = lax.all_to_all(shaped, "tensor", split_axis=2, concat_axis=0, tiled=True)
    moved = moved.reshape(blocks_all, repeat_count, local_blocks, token_count)
    return moved.transpose(2, 0, 1, 3).reshape(local_blocks, block_size, token_count)


def recompute(initial, factor_one, factor_two, gate_rows, layer_total):
    slot_count = factor_one.shape[0]
    hidden = initial
    saved = []
    for layer_slot in range(slot_count):
        first_out = jnp.einsum(
            "kij,mkjt->mkit", factor_one[layer_slot], hidden, preferred_element_type=jnp.float32
        ).astype(jnp.bfloat16)
        permuted = permute_blocks(first_out)
        mixed = jnp.einsum(
            "kij,mkjt->mkit", factor_two[layer_slot], permuted, preferred_element_type=jnp.float32
        )
        gate_now = gate_rows[layer_slot][None, :, :, None]
        next_hidden = (
            hidden.astype(jnp.float32) + gate_now * (mixed * jax.nn.sigmoid(mixed))
        ).astype(jnp.bfloat16)
        saved.append((hidden, permuted, mixed))
        hidden = jnp.where(layer_slot < layer_total, next_hidden, hidden)
    return saved


def shards(
    section_inputs, arriving_grad, loss_grad, factor_first, factor_second, gate_scales, layer_count
):
    moments = section_inputs.shape[1]
    slot_count = factor_first.shape[1]
    local_blocks = factor_first.shape[2]
    block_size = factor_first.shape[3]
    token_count = section_inputs.shape[3]
    first_local = factor_first[0]
    second_local = factor_second[0]
    gate_rows = gate_scales[0].reshape(slot_count, local_blocks, block_size)
    layer_total = layer_count[0]
    section_id = lax.axis_index("section")
    last_section = lax.axis_size("section") - 1
    inputs_local = section_inputs[0].reshape(moments, local_blocks, block_size, token_count)
    first_acc = [
        jnp.zeros((local_blocks, block_size, block_size), jnp.float32) for slot in range(slot_count)
    ]
    second_acc = [
        jnp.zeros((local_blocks, block_size, block_size), jnp.float32) for slot in range(slot_count)
    ]
    gate_acc = [jnp.zeros((local_blocks, block_size), jnp.float32) for slot in range(slot_count)]
    emitted = None
    for moment in range(moments):
        if moment == 0:
            arrived = arriving_grad[0].reshape(local_blocks, block_size, token_count)
        else:
            shifted = from_behind(emitted, "section", -1)
            from_loss = loss_grad[moment - 1].reshape(local_blocks, block_size, token_count)
            arrived = jnp.where(section_id == last_section, from_loss, shifted)
        computed = recompute(
            inputs_local[moment : moment + 1], first_local, second_local, gate_rows, layer_total
        )
        saved = [(record[0][0], record[1][0], record[2][0]) for record in computed]
        grad_now = arrived.astype(jnp.float32)
        for layer_slot in reversed(range(slot_count)):
            hidden, permuted, mixed = saved[layer_slot]
            is_live = layer_slot < layer_total
            logistic = jax.nn.sigmoid(mixed)
            gate_now = gate_rows[layer_slot][:, :, None]
            gate_term = jnp.sum(grad_now * (mixed * logistic), axis=2)
            gate_acc[layer_slot] = gate_acc[layer_slot] + jnp.where(
                is_live, gate_term, jnp.zeros_like(gate_term)
            )
            scaled = (grad_now * gate_now * logistic * (1.0 + mixed * (1.0 - logistic))).astype(
                jnp.bfloat16
            )
            backed = jnp.einsum(
                "kji,kjt->kit", second_local[layer_slot], scaled, preferred_element_type=jnp.float32
            ).astype(jnp.bfloat16)
            returned = unpermute_blocks(backed)
            moved_grad = grad_now + jnp.einsum(
                "kji,kjt->kit",
                first_local[layer_slot],
                returned,
                preferred_element_type=jnp.float32,
            )
            grad_now = jnp.where(is_live, moved_grad, grad_now)
            second_term = jnp.einsum(
                "kit,kjt->kij", scaled, permuted, preferred_element_type=jnp.float32
            )
            first_term = jnp.einsum(
                "kit,kjt->kij", returned, hidden, preferred_element_type=jnp.float32
            )
            second_acc[layer_slot] = second_acc[layer_slot] + jnp.where(
                is_live, second_term, jnp.zeros_like(second_term)
            )
            first_acc[layer_slot] = first_acc[layer_slot] + jnp.where(
                is_live, first_term, jnp.zeros_like(first_term)
            )
        emitted = grad_now.astype(jnp.bfloat16)
    last_emitted = emitted.reshape(1, local_blocks * block_size, token_count)
    gate_out = jnp.stack(gate_acc).reshape(1, slot_count, local_blocks * block_size)
    first_out = jnp.stack(first_acc).astype(jnp.bfloat16)[None]
    second_out = jnp.stack(second_acc).astype(jnp.bfloat16)[None]
    return (last_emitted, first_out, second_out, gate_out)


MESH = pl.DeviceIdType.MESH
F32 = jnp.float32
BF16 = jnp.bfloat16
CHUNKS = 4


def kernel(
    inp_far, arr_far, loss, one_far, two_far, gate_far, count_ref,
    emit_out, first_out, second_out, gate_out,
    inp, arr, one, two, one_t, two_t, gate, hid, perm, ret, send_f, send_b, work, slope, silu, gate_b, grad, gate_acc, scaled,
    hop_in, hop_out,
    recv_f, recv_b, sent_f, sent_b, hop_recv, hop_sent, loss_sem,
    inp_sem, one_sem, two_sem, far_sem,
):
    slots, blocks, size, tokens = one.shape
    rows = perm.shape[1]
    repeat = rows // blocks
    per = blocks // CHUNKS
    span = rows // CHUNKS
    me = lax.axis_index("tensor")
    section = lax.axis_index("section")
    last = lax.axis_size("section") - 1
    me_low, me_high = me % 2, me // 2

    def partner(d):
        low = 1 - me_low if d % 2 else me_low
        high = 1 - me_high if d // 2 else me_high
        return high * 2 + low

    def load_inp(t):
        return pltpu.make_async_copy(inp_far.at[t], inp.at[t], inp_sem.at[t])

    def load_one(l):
        return pltpu.make_async_copy(one_far.at[l], one.at[l], one_sem.at[l])

    def load_two(l):
        return pltpu.make_async_copy(two_far.at[l], two.at[l], two_sem.at[l])

    load_gate = pltpu.make_async_copy(gate_far, gate, far_sem.at[0])
    load_arr = pltpu.make_async_copy(arr_far, arr, far_sem.at[1])
    load_inp(0).start()
    load_one(0).start()
    load_inp(1).start()
    load_gate.start()
    for l in range(slots):
        load_two(l).start()
        if l:
            load_one(l).start()
    load_arr.start()

    barrier = pltpu.get_barrier_semaphore()
    for d in (1, 2, 3):
        pl.semaphore_signal(
            barrier, inc=1, device_id={"tensor": partner(d)}, device_id_type=MESH
        )

    @pl.when(section > 0)
    def _():
        pl.semaphore_signal(barrier, inc=1, device_id={"section": section - 1}, device_id_type=MESH)

    @pl.when(section < last)
    def _():
        pl.semaphore_signal(barrier, inc=1, device_id={"section": section + 1}, device_id_type=MESH)

    @pl.when(section == last)
    def _():
        pltpu.make_async_copy(loss, hop_in, loss_sem).start()

    count = count_ref[0]

    def hidden(t, l):
        return inp.at[t] if l == 0 else hid.at[t, l - 1]

    def step(t, l):
        return t * slots + l

    def dot(a, b):
        return jnp.dot(a, b, preferred_element_type=F32)


    def work_rows(k):
        return pl.ds(pl.multiple_of(k * size, size), size)

    def each_chunk(body, low=0, high=CHUNKS):
        lax.fori_loop(low, high, lambda c, _: (body(c), 0)[1], 0)

    def room(t, l):
        return 0 if t == 0 else 1 + l % 2

    def beside(chunk, early, late):
        def body(c):
            if early is not None:
                pl.when(c == CHUNKS // 2)(early)
            if late is not None:
                pl.when(c == CHUNKS - 1)(late)
            chunk(c)

        each_chunk(body)

    def each_block(body):
        def chunk(c):
            for b in range(per):
                body(c * per + b)

        each_chunk(chunk)

    def copy_f(f, d, c, source):
        part = pl.ds(c * span, span)
        return pltpu.make_async_remote_copy(
            src_ref=send_f.at[f, d - 1, part],
            dst_ref=perm.at[f, part, source],
            send_sem=sent_f.at[f, d - 1],
            recv_sem=recv_f.at[f, c, d - 1],
            device_id={"tensor": partner(d)},
            device_id_type=MESH,
        )

    def copy_b(f, h, d, c, source):
        part = pl.ds(c * per, per) if h else pl.ds(0, blocks)
        return pltpu.make_async_remote_copy(
            src_ref=send_b.at[f, d - 1, part, h],
            dst_ref=ret.at[f, part, source, h],
            send_sem=sent_b.at[f, d - 1],
            recv_sem=recv_b.at[f, c if h else CHUNKS, d - 1],
            device_id={"tensor": partner(d)},
            device_id_type=MESH,
        )

    def scatter_f(t, l, low=0, high=CHUNKS):
        f = step(t, l)

        def chunk(c):
            for d in (3, 1, 2, 0):
                target = partner(d)
                for j in range(span):
                    row = c * span + j
                    tile = work[
                        room(t, l), pl.ds(target * rows + row, blocks, stride=size), :
                    ].astype(BF16)
                    if d:
                        send_f[f, d - 1, row] = tile
                    else:
                        perm[f, row, me] = tile
                if d:
                    copy_f(f, d, c, me).start()

        each_chunk(chunk, low, high)

    def scatter_b(f, h):
        part = rows // 2
        pitch = size // repeat

        def chunk(c):
            for d in (3, 1, 2, 0):
                target = partner(d)
                for j in range(per):
                    block = c * per + j
                    tile = work[
                        0, pl.ds(h * part * pitch + target * blocks + block, part, stride=pitch), :
                    ].astype(BF16)
                    if d:
                        send_b[f, d - 1, block, h] = tile
                    else:
                        ret[f, block, me, h] = tile
                if d and h:
                    copy_b(f, h, d, c, me).start()

        each_chunk(chunk)
        if h == 0:
            for d in (3, 1, 2):
                copy_b(f, h, d, 0, me).start()

    def permuted(f, k):
        return perm[f, pl.ds(k * repeat, repeat)].reshape(size, tokens)

    def back(t, l, k, value):
        f = step(t, l)
        rounded = (value * slope[f, k]).astype(BF16)
        scaled[f, k] = rounded
        work[0, work_rows(k), :] = dot(two_t[l, k], rounded)
        grad[k] = value
        product = value * silu[f, k]
        gate_acc[l, k] = product if t == 0 else gate_acc[l, k] + product

    def forward(t, l, then, early=None, late=None, low=0, high=CHUNKS):
        f = step(t, l)

        def chunk(c):
            for d in (1, 2, 3):
                copy_f(f, d, c, partner(d)).wait_recv()
            for b in range(per):
                k = c * per + b
                mixed = dot(two[l, k], permuted(f, k))
                logistic = 0.5 + 0.5 * jnp.tanh(0.5 * mixed)
                branch = mixed * logistic
                scale = gate_b[l, k]
                if l + 1 < slots:
                    old = hidden(t, l)[k].astype(F32)
                    new = jnp.where(l < count, old + scale * branch, old).astype(BF16)
                    hid[t, l, k] = new
                    work[room(t, l + 1), work_rows(k), :] = dot(one[l + 1, k], new)
                silu[f, k] = branch
                slope[f, k] = scale * (logistic * (1.0 + mixed * (1.0 - logistic)))
                if then is not None:
                    then(k)

        if low or high < CHUNKS:
            each_chunk(chunk, low, high)
        else:
            beside(chunk, early, late)

    def backward(t, l, then, early=None, late=None):
        f = step(t, l)

        def chunk(c):
            @pl.when(c == 0)
            def _():
                for d in (1, 2, 3):
                    copy_b(f, 0, d, c, partner(d)).wait_recv()

            for d in (1, 2, 3):
                copy_b(f, 1, d, c, partner(d)).wait_recv()
            for b in range(per):
                k = c * per + b
                term = dot(one_t[l, k], ret[f, k].reshape(size, tokens))
                value = jnp.where(l < count, grad[k] + term, grad[k])
                then(k, value)
                if t == 1 and l == 0:
                    first_grad(0, k)
            if t == 0 and l == 0:
                hop_send(c)

        beside(chunk, early, late)

    def hop_copy(c):
        part = pl.ds(c * per, per)
        return pltpu.make_async_remote_copy(
            src_ref=hop_out.at[part],
            dst_ref=hop_in.at[part],
            send_sem=hop_sent.at[c],
            recv_sem=hop_recv.at[c],
            device_id={"section": section - 1},
            device_id_type=MESH,
        )

    def hop_send(c):
        @pl.when(section > 0)
        def _():
            hop_copy(c).start()

    def second_grads(l):
        f, g = step(0, l), step(1, l)

        def block(k):
            left = jnp.concatenate([scaled[f, k], scaled[g, k]], axis=1)
            right = jnp.concatenate([permuted(f, k), permuted(g, k)], axis=1)
            total = lax.dot_general(left, right, (((1,), (1,)), ((), ())), preferred_element_type=F32)
            second_out[l, k] = jnp.where(l < count, total, 0.0).astype(BF16)
            gates = jnp.sum(gate_acc[l, k].T, axis=0, keepdims=True)
            gate_out[l, pl.ds(k, 1), :] = jnp.where(l < count, gates, 0.0)

        each_block(block)

    def first_grad(l, k):
            f, g = step(0, l), step(1, l)
            left = jnp.concatenate(
                [ret[f, k].reshape(size, tokens), ret[g, k].reshape(size, tokens)], axis=1
            )
            right = jnp.concatenate([hidden(0, l)[k], hidden(1, l)[k]], axis=1)
            total = lax.dot_general(left, right, (((1,), (1,)), ((), ())), preferred_element_type=F32)
            first_out[l, k] = jnp.where(l < count, total, 0.0).astype(BF16)

    def first_grads(l):
        each_block(functools.partial(first_grad, l))

    def start(t):
        def block(k):
            work[room(t, 0), work_rows(k), :] = dot(one[0, k], inp[t, k])

        each_block(block)

    def widen(l):
        def block(k):
            gate_b[l, k] = jnp.broadcast_to(gate[l, pl.ds(k, 1), :], (size, size)).T

        each_block(block)

    def turn_over(source, target, l):
        def block(k):
            target[l, k] = source[l, k].T

        each_block(block)

    load_inp(0).wait()
    load_one(0).wait()
    start(0)
    pl.semaphore_wait(
        barrier, 3 + jnp.where(section > 0, 1, 0) + jnp.where(section < last, 1, 0)
    )
    scatter_f(0, 0)
    load_inp(1).wait()
    start(1)
    load_gate.wait()
    widen(0)
    load_two(0).wait()

    half = CHUNKS // 2
    halves = [(0, half), (half, CHUNKS)]
    turns = [(l, h) for l in range(slots) for h in halves]

    def receive(n):
        if n <= 0 or n > len(turns):
            return None
        l, (low, high) = turns[n - 1]
        return lambda: forward(1, l, None, low=low, high=high)

    def send(n):
        if n < 0 or n >= len(turns):
            return None
        l, (low, high) = turns[n]
        return lambda: scatter_f(1, l, low, high)

    def both(*calls):
        def run():
            for call in calls:
                if call is not None:
                    call()

        return run

    def ahead(t, l):
        return lambda: scatter_b(step(t, l), 0)

    top = slots - 1
    turn = -1
    for l in range(top):
        load_one(l + 1).wait()
        forward(0, l, None, receive(turn), send(turn))
        turn += 1
        scatter_f(0, l + 1)
        widen(l + 1)
        load_two(l + 1).wait()
    load_arr.wait()
    turn_over(two, two_t, top)
    forward(
        0, top, lambda k: back(0, top, k, arr[k].astype(F32)),
        both(ahead(0, top), receive(turn)), send(turn),
    )
    turn += 1
    scatter_b(step(0, top), 1)
    for l in range(top, 0, -1):
        turn_over(one, one_t, l)
        turn_over(two, two_t, l - 1)
        backward(
            0, l, functools.partial(back, 0, l - 1),
            both(ahead(0, l - 1), receive(turn)), send(turn),
        )
        turn += 1
        scatter_b(step(0, l - 1), 1)

    def leave(k, value):
        hop_out[k] = value.astype(BF16)

    turn_over(one, one_t, 0)
    backward(0, 0, leave, receive(turn), send(turn))
    turn += 1
    send(turn)()
    receive(turn)()
    turn += 1

    @pl.when(section == last)
    def _():
        pltpu.make_async_copy(loss, hop_in, loss_sem).wait()

    def arrive(c):
        @pl.when(section < last)
        def _():
            hop_copy(c).wait_recv()

        for b in range(per):
            k = c * per + b
            back(1, top, k, hop_in[k].astype(F32))

    beside(arrive, both(ahead(1, top), receive(turn)), None)
    scatter_b(step(1, top), 1)
    for l in range(top, 0, -1):
        second_grads(l)
        if l < top:
            first_grads(l + 1)
        backward(1, l, functools.partial(back, 1, l - 1), ahead(1, l - 1))
        scatter_b(step(1, l - 1), 1)
    second_grads(0)
    if top > 0:
        first_grads(1)

    def emit(k, value):
        emit_out[k] = value.astype(BF16)

    backward(1, 0, emit)

    for t in (0, 1):
        for l in range(slots):
            f = step(t, l)
            for d in (1, 2, 3):
                pltpu.make_async_remote_copy(
                    src_ref=send_f.at[f, d - 1], dst_ref=perm.at[f, :, me],
                    send_sem=sent_f.at[f, d - 1], recv_sem=recv_f.at[f, 0, d - 1],
                    device_id={"tensor": partner(d)}, device_id_type=MESH,
                ).wait_send()
                pltpu.make_async_remote_copy(
                    src_ref=send_b.at[f, d - 1], dst_ref=ret.at[f, :, me],
                    send_sem=sent_b.at[f, d - 1], recv_sem=recv_b.at[f, 0, d - 1],
                    device_id={"tensor": partner(d)}, device_id_type=MESH,
                ).wait_send()

    @pl.when(section > 0)
    def _():
        each_chunk(lambda c: hop_copy(c).wait_send())


def store_kernel(*refs):
    count = len(refs) // 2
    sems = refs[-1]
    copies = [
        pltpu.make_async_copy(refs[i], refs[count + i], sems.at[i]) for i in range(count)
    ]
    for copy in copies:
        copy.start()
    for copy in copies:
        copy.wait()


def store(values):
    return pl.pallas_call(
        store_kernel,
        out_shape=[jax.ShapeDtypeStruct(v.shape, v.dtype) for v in values],
        in_specs=[pl.BlockSpec(memory_space=pltpu.VMEM)] * len(values),
        out_specs=[pl.BlockSpec(memory_space=pl.ANY)] * len(values),
        scratch_shapes=[pltpu.SemaphoreType.DMA((len(values),))],
        compiler_params=pltpu.CompilerParams(vmem_limit_bytes=8 * 1024 * 1024),
    )(*values)


def fused_shards(
    section_inputs, arriving_grad, loss_grad, factor_first, factor_second, gate_scales, layer_count
):
    moments = section_inputs.shape[1]
    _, slots, blocks, size, _ = factor_first.shape
    tokens = section_inputs.shape[3]
    tensor = lax.axis_size("tensor")
    rows = size // tensor
    steps = moments * slots
    vmem = pl.BlockSpec(memory_space=pltpu.VMEM)
    block = (blocks, size, tokens)
    factor = (slots, blocks, size, size)
    outs = pl.pallas_call(
        kernel,
        out_shape=[
            pltpu.VMEM(block, BF16),
            pltpu.VMEM(factor, BF16),
            pltpu.VMEM(factor, BF16),
            pltpu.VMEM((slots, blocks, size), F32),
        ],
        in_specs=[pl.BlockSpec(memory_space=pl.ANY)] * 6 + [pl.BlockSpec(memory_space=pltpu.SMEM)],
        out_specs=[vmem] * 4,
        scratch_shapes=[
            pltpu.VMEM((moments,) + block, BF16),
            pltpu.VMEM(block, BF16),
            pltpu.VMEM(factor, BF16),
            pltpu.VMEM(factor, BF16),
            pltpu.VMEM(factor, BF16),
            pltpu.VMEM(factor, BF16),
            pltpu.VMEM((slots, blocks, size), F32),
            pltpu.VMEM((moments, max(slots - 1, 1)) + block, BF16),
            pltpu.VMEM((steps, rows, tensor, blocks, tokens), BF16),
            pltpu.VMEM((steps, blocks, tensor, 2, rows // 2, tokens), BF16),
            pltpu.VMEM((steps, 3, rows, blocks, tokens), BF16),
            pltpu.VMEM((steps, 3, blocks, 2, rows // 2, tokens), BF16),
            pltpu.VMEM((3, blocks * size, tokens), F32),
            pltpu.VMEM((steps,) + block, F32),
            pltpu.VMEM((steps,) + block, F32),
            pltpu.VMEM((slots,) + block, F32),
            pltpu.VMEM(block, F32),
            pltpu.VMEM((slots,) + block, F32),
            pltpu.VMEM((steps,) + block, BF16),
            pltpu.VMEM(block, BF16),
            pltpu.VMEM(block, BF16),
            pltpu.SemaphoreType.DMA((steps, CHUNKS, 3)),
            pltpu.SemaphoreType.DMA((steps, CHUNKS + 1, 3)),
            pltpu.SemaphoreType.DMA((steps, 3)),
            pltpu.SemaphoreType.DMA((steps, 3)),
            pltpu.SemaphoreType.DMA((CHUNKS,)),
            pltpu.SemaphoreType.DMA((CHUNKS,)),
            pltpu.SemaphoreType.DMA(()),
            pltpu.SemaphoreType.DMA((moments,)),
            pltpu.SemaphoreType.DMA((slots,)),
            pltpu.SemaphoreType.DMA((slots,)),
            pltpu.SemaphoreType.DMA((2,)),
        ],
        compiler_params=pltpu.CompilerParams(
            collective_id=0, has_side_effects=True, vmem_limit_bytes=56 * 1024 * 1024
        ),
    )(
        section_inputs[0].reshape((moments,) + block),
        arriving_grad[0].reshape(block),
        loss_grad[0].reshape(block),
        factor_first[0],
        factor_second[0],
        gate_scales[0].reshape(slots, blocks, size),
        layer_count,
    )
    emitted, first_grad, second_grad, gate_grad = store(outs)
    return (
        emitted.reshape(1, blocks * size, tokens),
        first_grad[None],
        second_grad[None],
        gate_grad.reshape(1, slots, blocks * size),
    )


def solution(mesh):
    in_specs = (
        P("section", None, "tensor", None),
        P("section", "tensor", None),
        P(None, "tensor", None),
        P("section", None, "tensor", None, None),
        P("section", None, "tensor", None, None),
        P("section", None, "tensor"),
        P("section"),
    )
    out_specs = (
        P("section", "tensor", None),
        P("section", None, "tensor", None, None),
        P("section", None, "tensor", None, None),
        P("section", None, "tensor"),
    )
    fused = mesh.shape["tensor"] == 4
    return jax.shard_map(fused_shards if fused else shards, mesh=mesh, in_specs=in_specs, out_specs=out_specs, check_vma=False)
```

```python
import functools

import jax
import jax.numpy as jnp
from jax import lax
from jax.experimental import pallas as pl
from jax.experimental.pallas import tpu as pltpu
from jax.sharding import PartitionSpec as P


def from_behind(value, axis, steps):
    count = lax.axis_size(axis)
    initial, last = (max(0, -steps), min(count, count - steps))
    return lax.ppermute(value, axis, [(source, source + steps) for source in range(initial, last)])


def permute_blocks(values):
    tensor_size = lax.axis_size("tensor")
    batch_count, local_blocks, block_size, token_count = values.shape
    blocks_all = local_blocks * tensor_size
    repeat_count = block_size // blocks_all
    shaped = values.reshape(
        batch_count, local_blocks, tensor_size, local_blocks, repeat_count, token_count
    )
    moved = lax.all_to_all(shaped, "tensor", split_axis=2, concat_axis=1, tiled=True)
    moved = moved.reshape(batch_count, blocks_all, local_blocks, repeat_count, token_count)
    return moved.transpose(0, 2, 3, 1, 4).reshape(
        batch_count, local_blocks, block_size, token_count
    )


def unpermute_blocks(values):
    tensor_size = lax.axis_size("tensor")
    local_blocks, block_size, token_count = values.shape
    blocks_all = local_blocks * tensor_size
    repeat_count = block_size // blocks_all
    shaped = values.reshape(local_blocks, repeat_count, tensor_size, local_blocks, token_count)
    moved = lax.all_to_all(shaped, "tensor", split_axis=2, concat_axis=0, tiled=True)
    moved = moved.reshape(blocks_all, repeat_count, local_blocks, token_count)
    return moved.transpose(2, 0, 1, 3).reshape(local_blocks, block_size, token_count)


def recompute(initial, factor_one, factor_two, gate_rows, layer_total):
    slot_count = factor_one.shape[0]
    hidden = initial
    saved = []
    for layer_slot in range(slot_count):
        first_out = jnp.einsum(
            "kij,mkjt->mkit", factor_one[layer_slot], hidden, preferred_element_type=jnp.float32
        ).astype(jnp.bfloat16)
        permuted = permute_blocks(first_out)
        mixed = jnp.einsum(
            "kij,mkjt->mkit", factor_two[layer_slot], permuted, preferred_element_type=jnp.float32
        )
        gate_now = gate_rows[layer_slot][None, :, :, None]
        next_hidden = (
            hidden.astype(jnp.float32) + gate_now * (mixed * jax.nn.sigmoid(mixed))
        ).astype(jnp.bfloat16)
        saved.append((hidden, permuted, mixed))
        hidden = jnp.where(layer_slot < layer_total, next_hidden, hidden)
    return saved


def shards(
    section_inputs, arriving_grad, loss_grad, factor_first, factor_second, gate_scales, layer_count
):
    moments = section_inputs.shape[1]
    slot_count = factor_first.shape[1]
    local_blocks = factor_first.shape[2]
    block_size = factor_first.shape[3]
    token_count = section_inputs.shape[3]
    first_local = factor_first[0]
    second_local = factor_second[0]
    gate_rows = gate_scales[0].reshape(slot_count, local_blocks, block_size)
    layer_total = layer_count[0]
    section_id = lax.axis_index("section")
    last_section = lax.axis_size("section") - 1
    inputs_local = section_inputs[0].reshape(moments, local_blocks, block_size, token_count)
    first_acc = [
        jnp.zeros((local_blocks, block_size, block_size), jnp.float32) for slot in range(slot_count)
    ]
    second_acc = [
        jnp.zeros((local_blocks, block_size, block_size), jnp.float32) for slot in range(slot_count)
    ]
    gate_acc = [jnp.zeros((local_blocks, block_size), jnp.float32) for slot in range(slot_count)]
    emitted = None
    for moment in range(moments):
        if moment == 0:
            arrived = arriving_grad[0].reshape(local_blocks, block_size, token_count)
        else:
            shifted = from_behind(emitted, "section", -1)
            from_loss = loss_grad[moment - 1].reshape(local_blocks, block_size, token_count)
            arrived = jnp.where(section_id == last_section, from_loss, shifted)
        computed = recompute(
            inputs_local[moment : moment + 1], first_local, second_local, gate_rows, layer_total
        )
        saved = [(record[0][0], record[1][0], record[2][0]) for record in computed]
        grad_now = arrived.astype(jnp.float32)
        for layer_slot in reversed(range(slot_count)):
            hidden, permuted, mixed = saved[layer_slot]
            is_live = layer_slot < layer_total
            logistic = jax.nn.sigmoid(mixed)
            gate_now = gate_rows[layer_slot][:, :, None]
            gate_term = jnp.sum(grad_now * (mixed * logistic), axis=2)
            gate_acc[layer_slot] = gate_acc[layer_slot] + jnp.where(
                is_live, gate_term, jnp.zeros_like(gate_term)
            )
            scaled = (grad_now * gate_now * logistic * (1.0 + mixed * (1.0 - logistic))).astype(
                jnp.bfloat16
            )
            backed = jnp.einsum(
                "kji,kjt->kit", second_local[layer_slot], scaled, preferred_element_type=jnp.float32
            ).astype(jnp.bfloat16)
            returned = unpermute_blocks(backed)
            moved_grad = grad_now + jnp.einsum(
                "kji,kjt->kit",
                first_local[layer_slot],
                returned,
                preferred_element_type=jnp.float32,
            )
            grad_now = jnp.where(is_live, moved_grad, grad_now)
            second_term = jnp.einsum(
                "kit,kjt->kij", scaled, permuted, preferred_element_type=jnp.float32
            )
            first_term = jnp.einsum(
                "kit,kjt->kij", returned, hidden, preferred_element_type=jnp.float32
            )
            second_acc[layer_slot] = second_acc[layer_slot] + jnp.where(
                is_live, second_term, jnp.zeros_like(second_term)
            )
            first_acc[layer_slot] = first_acc[layer_slot] + jnp.where(
                is_live, first_term, jnp.zeros_like(first_term)
            )
        emitted = grad_now.astype(jnp.bfloat16)
    last_emitted = emitted.reshape(1, local_blocks * block_size, token_count)
    gate_out = jnp.stack(gate_acc).reshape(1, slot_count, local_blocks * block_size)
    first_out = jnp.stack(first_acc).astype(jnp.bfloat16)[None]
    second_out = jnp.stack(second_acc).astype(jnp.bfloat16)[None]
    return (last_emitted, first_out, second_out, gate_out)


MESH = pl.DeviceIdType.MESH
F32 = jnp.float32
BF16 = jnp.bfloat16
CHUNKS = 4


def kernel(
    inp_far, arr_far, loss, one_far, two_far, gate_far, count_ref,
    emit_out, first_out, second_out, gate_out,
    inp, arr, one, two, one_t, two_t, gate, hid, perm, ret, send_f, send_b, work, slope, silu, gate_b, grad, gate_acc, scaled,
    hop_in, hop_out,
    recv_f, recv_b, sent_f, sent_b, hop_recv, hop_sent, loss_sem,
    inp_sem, one_sem, two_sem, far_sem,
):
    slots, blocks, size, tokens = one.shape
    rows = perm.shape[1]
    repeat = rows // blocks
    per = blocks // CHUNKS
    span = rows // CHUNKS
    me = lax.axis_index("tensor")
    section = lax.axis_index("section")
    last = lax.axis_size("section") - 1
    me_low, me_high = me % 2, me // 2

    def partner(d):
        low = 1 - me_low if d % 2 else me_low
        high = 1 - me_high if d // 2 else me_high
        return high * 2 + low

    def load_inp(t):
        return pltpu.make_async_copy(inp_far.at[t], inp.at[t], inp_sem.at[t])

    def load_one(l):
        return pltpu.make_async_copy(one_far.at[l], one.at[l], one_sem.at[l])

    def load_two(l):
        return pltpu.make_async_copy(two_far.at[l], two.at[l], two_sem.at[l])

    load_gate = pltpu.make_async_copy(gate_far, gate, far_sem.at[0])
    load_arr = pltpu.make_async_copy(arr_far, arr, far_sem.at[1])
    load_inp(0).start()
    load_one(0).start()
    load_inp(1).start()
    load_gate.start()
    for l in range(slots):
        load_two(l).start()
        if l:
            load_one(l).start()
    load_arr.start()

    barrier = pltpu.get_barrier_semaphore()
    for d in (1, 2, 3):
        pl.semaphore_signal(
            barrier, inc=1, device_id={"tensor": partner(d)}, device_id_type=MESH
        )

    @pl.when(section > 0)
    def _():
        pl.semaphore_signal(barrier, inc=1, device_id={"section": section - 1}, device_id_type=MESH)

    @pl.when(section < last)
    def _():
        pl.semaphore_signal(barrier, inc=1, device_id={"section": section + 1}, device_id_type=MESH)

    @pl.when(section == last)
    def _():
        pltpu.make_async_copy(loss, hop_in, loss_sem).start()

    count = count_ref[0]

    def hidden(t, l):
        return inp.at[t] if l == 0 else hid.at[t, l - 1]

    def step(t, l):
        return t * slots + l

    def dot(a, b):
        return jnp.dot(a, b, preferred_element_type=F32)


    def work_rows(k):
        return pl.ds(pl.multiple_of(k * size, size), size)

    def each_chunk(body, low=0, high=CHUNKS):
        lax.fori_loop(low, high, lambda c, _: (body(c), 0)[1], 0)

    def room(t, l):
        return 0 if t == 0 else 1 + l % 2

    def beside(chunk, early, late):
        def body(c):
            if early is not None:
                pl.when(c == CHUNKS // 2)(early)
            if late is not None:
                pl.when(c == CHUNKS - 1)(late)
            chunk(c)

        each_chunk(body)

    def each_block(body):
        def chunk(c):
            for b in range(per):
                body(c * per + b)

        each_chunk(chunk)

    def copy_f(f, d, c, source):
        part = pl.ds(c * span, span)
        return pltpu.make_async_remote_copy(
            src_ref=send_f.at[f, d - 1, part],
            dst_ref=perm.at[f, part, source],
            send_sem=sent_f.at[f, d - 1],
            recv_sem=recv_f.at[f, c, d - 1],
            device_id={"tensor": partner(d)},
            device_id_type=MESH,
        )

    def copy_b(f, h, d, c, source):
        part = pl.ds(c * per, per) if h else pl.ds(0, blocks)
        return pltpu.make_async_remote_copy(
            src_ref=send_b.at[f, d - 1, part, h],
            dst_ref=ret.at[f, part, source, h],
            send_sem=sent_b.at[f, d - 1],
            recv_sem=recv_b.at[f, c if h else CHUNKS, d - 1],
            device_id={"tensor": partner(d)},
            device_id_type=MESH,
        )

    def scatter_f(t, l, low=0, high=CHUNKS):
        f = step(t, l)

        def chunk(c):
            for d in (3, 1, 2, 0):
                target = partner(d)
                for j in range(span):
                    row = c * span + j
                    tile = work[
                        room(t, l), pl.ds(target * rows + row, blocks, stride=size), :
                    ].astype(BF16)
                    if d:
                        send_f[f, d - 1, row] = tile
                    else:
                        perm[f, row, me] = tile
                if d:
                    copy_f(f, d, c, me).start()

        each_chunk(chunk, low, high)

    def scatter_b(f, h):
        part = rows // 2
        pitch = size // repeat

        def chunk(c):
            for d in (3, 1, 2, 0):
                target = partner(d)
                for j in range(per):
                    block = c * per + j
                    tile = work[
                        0, pl.ds(h * part * pitch + target * blocks + block, part, stride=pitch), :
                    ].astype(BF16)
                    if d:
                        send_b[f, d - 1, block, h] = tile
                    else:
                        ret[f, block, me, h] = tile
                if d and h:
                    copy_b(f, h, d, c, me).start()

        each_chunk(chunk)
        if h == 0:
            for d in (3, 1, 2):
                copy_b(f, h, d, 0, me).start()

    def permuted(f, k):
        return perm[f, pl.ds(k * repeat, repeat)].reshape(size, tokens)

    def back(t, l, k, value):
        f = step(t, l)
        rounded = (value * slope[f, k]).astype(BF16)
        scaled[f, k] = rounded
        work[0, work_rows(k), :] = dot(two_t[l, k], rounded)
        grad[k] = value
        product = value * silu[f, k]
        gate_acc[l, k] = product if t == 0 else gate_acc[l, k] + product

    def forward(t, l, then, early=None, late=None, low=0, high=CHUNKS):
        f = step(t, l)

        def chunk(c):
            for d in (1, 2, 3):
                copy_f(f, d, c, partner(d)).wait_recv()
            for b in range(per):
                k = c * per + b
                mixed = dot(two[l, k], permuted(f, k))
                logistic = 0.5 + 0.5 * jnp.tanh(0.5 * mixed)
                branch = mixed * logistic
                scale = gate_b[l, k]
                if l + 1 < slots:
                    old = hidden(t, l)[k].astype(F32)
                    new = jnp.where(l < count, old + scale * branch, old).astype(BF16)
                    hid[t, l, k] = new
                    work[room(t, l + 1), work_rows(k), :] = dot(one[l + 1, k], new)
                silu[f, k] = branch
                slope[f, k] = scale * (logistic * (1.0 + mixed * (1.0 - logistic)))
                if then is not None:
                    then(k)

        if low or high < CHUNKS:
            each_chunk(chunk, low, high)
        else:
            beside(chunk, early, late)

    def backward(t, l, then, early=None, late=None):
        f = step(t, l)

        def chunk(c):
            @pl.when(c == 0)
            def _():
                for d in (1, 2, 3):
                    copy_b(f, 0, d, c, partner(d)).wait_recv()

            for d in (1, 2, 3):
                copy_b(f, 1, d, c, partner(d)).wait_recv()
            for b in range(per):
                k = c * per + b
                term = dot(one_t[l, k], ret[f, k].reshape(size, tokens))
                value = jnp.where(l < count, grad[k] + term, grad[k])
                then(k, value)
                if t == 1 and l == 0:
                    first_grad(0, k)
            if t == 0 and l == 0:
                hop_send(c)

        beside(chunk, early, late)

    def hop_copy(c):
        part = pl.ds(c * per, per)
        return pltpu.make_async_remote_copy(
            src_ref=hop_out.at[part],
            dst_ref=hop_in.at[part],
            send_sem=hop_sent.at[c],
            recv_sem=hop_recv.at[c],
            device_id={"section": section - 1},
            device_id_type=MESH,
        )

    def hop_send(c):
        @pl.when(section > 0)
        def _():
            hop_copy(c).start()

    def second_grads(l):
        f, g = step(0, l), step(1, l)

        def block(k):
            left = jnp.concatenate([scaled[f, k], scaled[g, k]], axis=1)
            right = jnp.concatenate([permuted(f, k), permuted(g, k)], axis=1)
            total = lax.dot_general(left, right, (((1,), (1,)), ((), ())), preferred_element_type=F32)
            second_out[l, k] = jnp.where(l < count, total, 0.0).astype(BF16)
            gates = jnp.sum(gate_acc[l, k].T, axis=0, keepdims=True)
            gate_out[l, pl.ds(k, 1), :] = jnp.where(l < count, gates, 0.0)

        each_block(block)

    def first_grad(l, k):
            f, g = step(0, l), step(1, l)
            left = jnp.concatenate(
                [ret[f, k].reshape(size, tokens), ret[g, k].reshape(size, tokens)], axis=1
            )
            right = jnp.concatenate([hidden(0, l)[k], hidden(1, l)[k]], axis=1)
            total = lax.dot_general(left, right, (((1,), (1,)), ((), ())), preferred_element_type=F32)
            first_out[l, k] = jnp.where(l < count, total, 0.0).astype(BF16)

    def first_grads(l):
        each_block(functools.partial(first_grad, l))

    def start(t):
        def block(k):
            work[room(t, 0), work_rows(k), :] = dot(one[0, k], inp[t, k])

        each_block(block)

    def widen(l):
        def block(k):
            gate_b[l, k] = jnp.broadcast_to(gate[l, pl.ds(k, 1), :], (size, size)).T

        each_block(block)

    def turn_over(source, target, l):
        def block(k):
            target[l, k] = source[l, k].T

        each_block(block)

    load_inp(0).wait()
    load_one(0).wait()
    start(0)
    pl.semaphore_wait(
        barrier, 3 + jnp.where(section > 0, 1, 0) + jnp.where(section < last, 1, 0)
    )
    scatter_f(0, 0)
    load_inp(1).wait()
    start(1)
    load_gate.wait()
    widen(0)
    load_two(0).wait()

    half = CHUNKS // 2
    halves = [(0, half), (half, CHUNKS)]
    turns = [(l, h) for l in range(slots) for h in halves]

    pause = len(turns) - 2

    def receive(n):
        if n <= 0 or n == pause + 1:
            return None
        l, (low, high) = turns[n - 1 if n <= pause else n - 2]
        return lambda: forward(1, l, None, low=low, high=high)

    def send(n):
        if n == pause:
            return None
        l, (low, high) = turns[n if n < pause else n - 1]
        return lambda: scatter_f(1, l, low, high)

    def both(*calls):
        def run():
            for call in calls:
                if call is not None:
                    call()

        return run

    def ahead(t, l):
        return lambda: scatter_b(step(t, l), 0)

    top = slots - 1
    turn = 0
    for l in range(top):
        load_one(l + 1).wait()
        forward(0, l, None, receive(turn), send(turn))
        turn += 1
        scatter_f(0, l + 1)
        widen(l + 1)
        load_two(l + 1).wait()
    load_arr.wait()
    turn_over(two, two_t, top)
    forward(
        0, top, lambda k: back(0, top, k, arr[k].astype(F32)),
        both(ahead(0, top), receive(turn)), send(turn),
    )
    turn += 1
    scatter_b(step(0, top), 1)
    for l in range(top, 0, -1):
        turn_over(one, one_t, l)
        turn_over(two, two_t, l - 1)
        backward(
            0, l, functools.partial(back, 0, l - 1),
            both(ahead(0, l - 1), receive(turn)), send(turn),
        )
        turn += 1
        scatter_b(step(0, l - 1), 1)

    def leave(k, value):
        hop_out[k] = value.astype(BF16)

    turn_over(one, one_t, 0)
    backward(0, 0, leave, receive(turn), send(turn))
    turn += 1
    send(turn)()
    receive(turn)()
    turn += 1

    @pl.when(section == last)
    def _():
        pltpu.make_async_copy(loss, hop_in, loss_sem).wait()

    def arrive(c):
        @pl.when(section < last)
        def _():
            hop_copy(c).wait_recv()

        for b in range(per):
            k = c * per + b
            back(1, top, k, hop_in[k].astype(F32))

    beside(arrive, both(ahead(1, top), receive(turn)), None)
    scatter_b(step(1, top), 1)
    for l in range(top, 0, -1):
        second_grads(l)
        if l < top:
            first_grads(l + 1)
        backward(1, l, functools.partial(back, 1, l - 1), ahead(1, l - 1))
        scatter_b(step(1, l - 1), 1)
    second_grads(0)
    if top > 0:
        first_grads(1)

    def emit(k, value):
        emit_out[k] = value.astype(BF16)

    backward(1, 0, emit)

    for t in (0, 1):
        for l in range(slots):
            f = step(t, l)
            for d in (1, 2, 3):
                pltpu.make_async_remote_copy(
                    src_ref=send_f.at[f, d - 1], dst_ref=perm.at[f, :, me],
                    send_sem=sent_f.at[f, d - 1], recv_sem=recv_f.at[f, 0, d - 1],
                    device_id={"tensor": partner(d)}, device_id_type=MESH,
                ).wait_send()
                pltpu.make_async_remote_copy(
                    src_ref=send_b.at[f, d - 1], dst_ref=ret.at[f, :, me],
                    send_sem=sent_b.at[f, d - 1], recv_sem=recv_b.at[f, 0, d - 1],
                    device_id={"tensor": partner(d)}, device_id_type=MESH,
                ).wait_send()

    @pl.when(section > 0)
    def _():
        each_chunk(lambda c: hop_copy(c).wait_send())


def store_kernel(*refs):
    count = len(refs) // 2
    sems = refs[-1]
    copies = [
        pltpu.make_async_copy(refs[i], refs[count + i], sems.at[i]) for i in range(count)
    ]
    for copy in copies:
        copy.start()
    for copy in copies:
        copy.wait()


def store(values):
    return pl.pallas_call(
        store_kernel,
        out_shape=[jax.ShapeDtypeStruct(v.shape, v.dtype) for v in values],
        in_specs=[pl.BlockSpec(memory_space=pltpu.VMEM)] * len(values),
        out_specs=[pl.BlockSpec(memory_space=pl.ANY)] * len(values),
        scratch_shapes=[pltpu.SemaphoreType.DMA((len(values),))],
        compiler_params=pltpu.CompilerParams(vmem_limit_bytes=8 * 1024 * 1024),
    )(*values)


def fused_shards(
    section_inputs, arriving_grad, loss_grad, factor_first, factor_second, gate_scales, layer_count
):
    moments = section_inputs.shape[1]
    _, slots, blocks, size, _ = factor_first.shape
    tokens = section_inputs.shape[3]
    tensor = lax.axis_size("tensor")
    rows = size // tensor
    steps = moments * slots
    vmem = pl.BlockSpec(memory_space=pltpu.VMEM)
    block = (blocks, size, tokens)
    factor = (slots, blocks, size, size)
    outs = pl.pallas_call(
        kernel,
        out_shape=[
            pltpu.VMEM(block, BF16),
            pltpu.VMEM(factor, BF16),
            pltpu.VMEM(factor, BF16),
            pltpu.VMEM((slots, blocks, size), F32),
        ],
        in_specs=[pl.BlockSpec(memory_space=pl.ANY)] * 6 + [pl.BlockSpec(memory_space=pltpu.SMEM)],
        out_specs=[vmem] * 4,
        scratch_shapes=[
            pltpu.VMEM((moments,) + block, BF16),
            pltpu.VMEM(block, BF16),
            pltpu.VMEM(factor, BF16),
            pltpu.VMEM(factor, BF16),
            pltpu.VMEM(factor, BF16),
            pltpu.VMEM(factor, BF16),
            pltpu.VMEM((slots, blocks, size), F32),
            pltpu.VMEM((moments, max(slots - 1, 1)) + block, BF16),
            pltpu.VMEM((steps, rows, tensor, blocks, tokens), BF16),
            pltpu.VMEM((steps, blocks, tensor, 2, rows // 2, tokens), BF16),
            pltpu.VMEM((steps, 3, rows, blocks, tokens), BF16),
            pltpu.VMEM((steps, 3, blocks, 2, rows // 2, tokens), BF16),
            pltpu.VMEM((3, blocks * size, tokens), F32),
            pltpu.VMEM((steps,) + block, F32),
            pltpu.VMEM((steps,) + block, F32),
            pltpu.VMEM((slots,) + block, F32),
            pltpu.VMEM(block, F32),
            pltpu.VMEM((slots,) + block, F32),
            pltpu.VMEM((steps,) + block, BF16),
            pltpu.VMEM(block, BF16),
            pltpu.VMEM(block, BF16),
            pltpu.SemaphoreType.DMA((steps, CHUNKS, 3)),
            pltpu.SemaphoreType.DMA((steps, CHUNKS + 1, 3)),
            pltpu.SemaphoreType.DMA((steps, 3)),
            pltpu.SemaphoreType.DMA((steps, 3)),
            pltpu.SemaphoreType.DMA((CHUNKS,)),
            pltpu.SemaphoreType.DMA((CHUNKS,)),
            pltpu.SemaphoreType.DMA(()),
            pltpu.SemaphoreType.DMA((moments,)),
            pltpu.SemaphoreType.DMA((slots,)),
            pltpu.SemaphoreType.DMA((slots,)),
            pltpu.SemaphoreType.DMA((2,)),
        ],
        compiler_params=pltpu.CompilerParams(
            collective_id=0, has_side_effects=True, vmem_limit_bytes=56 * 1024 * 1024
        ),
    )(
        section_inputs[0].reshape((moments,) + block),
        arriving_grad[0].reshape(block),
        loss_grad[0].reshape(block),
        factor_first[0],
        factor_second[0],
        gate_scales[0].reshape(slots, blocks, size),
        layer_count,
    )
    emitted, first_grad, second_grad, gate_grad = store(outs)
    return (
        emitted.reshape(1, blocks * size, tokens),
        first_grad[None],
        second_grad[None],
        gate_grad.reshape(1, slots, blocks * size),
    )


def solution(mesh):
    in_specs = (
        P("section", None, "tensor", None),
        P("section", "tensor", None),
        P(None, "tensor", None),
        P("section", None, "tensor", None, None),
        P("section", None, "tensor", None, None),
        P("section", None, "tensor"),
        P("section"),
    )
    out_specs = (
        P("section", "tensor", None),
        P("section", None, "tensor", None, None),
        P("section", None, "tensor", None, None),
        P("section", None, "tensor"),
    )
    fused = mesh.shape["tensor"] == 4
    return jax.shard_map(fused_shards if fused else shards, mesh=mesh, in_specs=in_specs, out_specs=out_specs, check_vma=False)
```

```python
import functools

import jax
import jax.numpy as jnp
from jax import lax
from jax.experimental import pallas as pl
from jax.experimental.pallas import tpu as pltpu
from jax.sharding import PartitionSpec as P


def from_behind(value, axis, steps):
    count = lax.axis_size(axis)
    initial, last = (max(0, -steps), min(count, count - steps))
    return lax.ppermute(value, axis, [(source, source + steps) for source in range(initial, last)])


def permute_blocks(values):
    tensor_size = lax.axis_size("tensor")
    batch_count, local_blocks, block_size, token_count = values.shape
    blocks_all = local_blocks * tensor_size
    repeat_count = block_size // blocks_all
    shaped = values.reshape(
        batch_count, local_blocks, tensor_size, local_blocks, repeat_count, token_count
    )
    moved = lax.all_to_all(shaped, "tensor", split_axis=2, concat_axis=1, tiled=True)
    moved = moved.reshape(batch_count, blocks_all, local_blocks, repeat_count, token_count)
    return moved.transpose(0, 2, 3, 1, 4).reshape(
        batch_count, local_blocks, block_size, token_count
    )


def unpermute_blocks(values):
    tensor_size = lax.axis_size("tensor")
    local_blocks, block_size, token_count = values.shape
    blocks_all = local_blocks * tensor_size
    repeat_count = block_size // blocks_all
    shaped = values.reshape(local_blocks, repeat_count, tensor_size, local_blocks, token_count)
    moved = lax.all_to_all(shaped, "tensor", split_axis=2, concat_axis=0, tiled=True)
    moved = moved.reshape(blocks_all, repeat_count, local_blocks, token_count)
    return moved.transpose(2, 0, 1, 3).reshape(local_blocks, block_size, token_count)


def recompute(initial, factor_one, factor_two, gate_rows, layer_total):
    slot_count = factor_one.shape[0]
    hidden = initial
    saved = []
    for layer_slot in range(slot_count):
        first_out = jnp.einsum(
            "kij,mkjt->mkit", factor_one[layer_slot], hidden, preferred_element_type=jnp.float32
        ).astype(jnp.bfloat16)
        permuted = permute_blocks(first_out)
        mixed = jnp.einsum(
            "kij,mkjt->mkit", factor_two[layer_slot], permuted, preferred_element_type=jnp.float32
        )
        gate_now = gate_rows[layer_slot][None, :, :, None]
        next_hidden = (
            hidden.astype(jnp.float32) + gate_now * (mixed * jax.nn.sigmoid(mixed))
        ).astype(jnp.bfloat16)
        saved.append((hidden, permuted, mixed))
        hidden = jnp.where(layer_slot < layer_total, next_hidden, hidden)
    return saved


def shards(
    section_inputs, arriving_grad, loss_grad, factor_first, factor_second, gate_scales, layer_count
):
    moments = section_inputs.shape[1]
    slot_count = factor_first.shape[1]
    local_blocks = factor_first.shape[2]
    block_size = factor_first.shape[3]
    token_count = section_inputs.shape[3]
    first_local = factor_first[0]
    second_local = factor_second[0]
    gate_rows = gate_scales[0].reshape(slot_count, local_blocks, block_size)
    layer_total = layer_count[0]
    section_id = lax.axis_index("section")
    last_section = lax.axis_size("section") - 1
    inputs_local = section_inputs[0].reshape(moments, local_blocks, block_size, token_count)
    first_acc = [
        jnp.zeros((local_blocks, block_size, block_size), jnp.float32) for slot in range(slot_count)
    ]
    second_acc = [
        jnp.zeros((local_blocks, block_size, block_size), jnp.float32) for slot in range(slot_count)
    ]
    gate_acc = [jnp.zeros((local_blocks, block_size), jnp.float32) for slot in range(slot_count)]
    emitted = None
    for moment in range(moments):
        if moment == 0:
            arrived = arriving_grad[0].reshape(local_blocks, block_size, token_count)
        else:
            shifted = from_behind(emitted, "section", -1)
            from_loss = loss_grad[moment - 1].reshape(local_blocks, block_size, token_count)
            arrived = jnp.where(section_id == last_section, from_loss, shifted)
        computed = recompute(
            inputs_local[moment : moment + 1], first_local, second_local, gate_rows, layer_total
        )
        saved = [(record[0][0], record[1][0], record[2][0]) for record in computed]
        grad_now = arrived.astype(jnp.float32)
        for layer_slot in reversed(range(slot_count)):
            hidden, permuted, mixed = saved[layer_slot]
            is_live = layer_slot < layer_total
            logistic = jax.nn.sigmoid(mixed)
            gate_now = gate_rows[layer_slot][:, :, None]
            gate_term = jnp.sum(grad_now * (mixed * logistic), axis=2)
            gate_acc[layer_slot] = gate_acc[layer_slot] + jnp.where(
                is_live, gate_term, jnp.zeros_like(gate_term)
            )
            scaled = (grad_now * gate_now * logistic * (1.0 + mixed * (1.0 - logistic))).astype(
                jnp.bfloat16
            )
            backed = jnp.einsum(
                "kji,kjt->kit", second_local[layer_slot], scaled, preferred_element_type=jnp.float32
            ).astype(jnp.bfloat16)
            returned = unpermute_blocks(backed)
            moved_grad = grad_now + jnp.einsum(
                "kji,kjt->kit",
                first_local[layer_slot],
                returned,
                preferred_element_type=jnp.float32,
            )
            grad_now = jnp.where(is_live, moved_grad, grad_now)
            second_term = jnp.einsum(
                "kit,kjt->kij", scaled, permuted, preferred_element_type=jnp.float32
            )
            first_term = jnp.einsum(
                "kit,kjt->kij", returned, hidden, preferred_element_type=jnp.float32
            )
            second_acc[layer_slot] = second_acc[layer_slot] + jnp.where(
                is_live, second_term, jnp.zeros_like(second_term)
            )
            first_acc[layer_slot] = first_acc[layer_slot] + jnp.where(
                is_live, first_term, jnp.zeros_like(first_term)
            )
        emitted = grad_now.astype(jnp.bfloat16)
    last_emitted = emitted.reshape(1, local_blocks * block_size, token_count)
    gate_out = jnp.stack(gate_acc).reshape(1, slot_count, local_blocks * block_size)
    first_out = jnp.stack(first_acc).astype(jnp.bfloat16)[None]
    second_out = jnp.stack(second_acc).astype(jnp.bfloat16)[None]
    return (last_emitted, first_out, second_out, gate_out)


MESH = pl.DeviceIdType.MESH
F32 = jnp.float32
BF16 = jnp.bfloat16
CHUNKS = 4


def kernel(
    inp_far, arr_far, loss, one_far, two_far, gate_far, count_ref,
    emit_out, first_out, second_out, gate_out,
    inp, arr, one, two, one_t, two_t, gate, hid, perm, ret, send_f, send_b, work, slope, silu, gate_b, grad, gate_acc, scaled,
    hop_in, hop_out,
    recv_f, recv_b, sent_f, sent_b, hop_recv, hop_sent, loss_sem,
    inp_sem, one_sem, two_sem, far_sem,
):
    slots, blocks, size, tokens = one.shape
    rows = perm.shape[1]
    repeat = rows // blocks
    per = blocks // CHUNKS
    span = rows // CHUNKS
    me = lax.axis_index("tensor")
    section = lax.axis_index("section")
    last = lax.axis_size("section") - 1
    me_low, me_high = me % 2, me // 2

    def partner(d):
        low = 1 - me_low if d % 2 else me_low
        high = 1 - me_high if d // 2 else me_high
        return high * 2 + low

    def load_inp(t):
        return pltpu.make_async_copy(inp_far.at[t], inp.at[t], inp_sem.at[t])

    def load_one(l):
        return pltpu.make_async_copy(one_far.at[l], one.at[l], one_sem.at[l])

    def load_two(l):
        return pltpu.make_async_copy(two_far.at[l], two.at[l], two_sem.at[l])

    load_gate = pltpu.make_async_copy(gate_far, gate, far_sem.at[0])
    load_arr = pltpu.make_async_copy(arr_far, arr, far_sem.at[1])
    load_inp(0).start()
    load_one(0).start()
    load_inp(1).start()
    load_gate.start()
    for l in range(slots):
        load_two(l).start()
        if l:
            load_one(l).start()
    load_arr.start()

    barrier = pltpu.get_barrier_semaphore()
    for d in (1, 2, 3):
        pl.semaphore_signal(
            barrier, inc=1, device_id={"tensor": partner(d)}, device_id_type=MESH
        )

    @pl.when(section > 0)
    def _():
        pl.semaphore_signal(barrier, inc=1, device_id={"section": section - 1}, device_id_type=MESH)

    @pl.when(section < last)
    def _():
        pl.semaphore_signal(barrier, inc=1, device_id={"section": section + 1}, device_id_type=MESH)

    @pl.when(section == last)
    def _():
        pltpu.make_async_copy(loss, hop_in, loss_sem).start()

    count = count_ref[0]

    def hidden(t, l):
        return inp.at[t] if l == 0 else hid.at[t, l - 1]

    def step(t, l):
        return t * slots + l

    def dot(a, b):
        return jnp.dot(a, b, preferred_element_type=F32)


    def work_rows(k):
        return pl.ds(pl.multiple_of(k * size, size), size)

    def each_chunk(body, low=0, high=CHUNKS):
        lax.fori_loop(low, high, lambda c, _: (body(c), 0)[1], 0)

    def room(t, l):
        return 0 if t == 0 else 1 + l % 2

    def beside(chunk, early, late):
        def body(c):
            if early is not None:
                pl.when(c == CHUNKS // 2)(early)
            if late is not None:
                pl.when(c == CHUNKS - 1)(late)
            chunk(c)

        each_chunk(body)

    def each_block(body):
        def chunk(c):
            for b in range(per):
                body(c * per + b)

        each_chunk(chunk)

    def copy_f(f, d, c, source):
        part = pl.ds(c * span, span)
        return pltpu.make_async_remote_copy(
            src_ref=send_f.at[f, d - 1, part],
            dst_ref=perm.at[f, part, source],
            send_sem=sent_f.at[f, d - 1],
            recv_sem=recv_f.at[f, c, d - 1],
            device_id={"tensor": partner(d)},
            device_id_type=MESH,
        )

    def copy_b(f, h, d, c, source):
        part = pl.ds(c * per, per) if h else pl.ds(0, blocks)
        return pltpu.make_async_remote_copy(
            src_ref=send_b.at[f, d - 1, part, h],
            dst_ref=ret.at[f, part, source, h],
            send_sem=sent_b.at[f, d - 1],
            recv_sem=recv_b.at[f, c if h else CHUNKS, d - 1],
            device_id={"tensor": partner(d)},
            device_id_type=MESH,
        )

    def scatter_f(t, l, low=0, high=CHUNKS):
        f = step(t, l)

        def chunk(c):
            for d in (3, 1, 2, 0):
                target = partner(d)
                for j in range(span):
                    row = c * span + j
                    tile = work[
                        room(t, l), pl.ds(target * rows + row, blocks, stride=size), :
                    ].astype(BF16)
                    if d:
                        send_f[f, d - 1, row] = tile
                    else:
                        perm[f, row, me] = tile
                if d:
                    copy_f(f, d, c, me).start()

        each_chunk(chunk, low, high)

    def scatter_b(f, h):
        part = rows // 2
        pitch = size // repeat

        def chunk(c):
            for d in (3, 1, 2, 0):
                target = partner(d)
                for j in range(per):
                    block = c * per + j
                    tile = work[
                        0, pl.ds(h * part * pitch + target * blocks + block, part, stride=pitch), :
                    ].astype(BF16)
                    if d:
                        send_b[f, d - 1, block, h] = tile
                    else:
                        ret[f, block, me, h] = tile
                if d and h:
                    copy_b(f, h, d, c, me).start()

        each_chunk(chunk)
        if h == 0:
            for d in (3, 1, 2):
                copy_b(f, h, d, 0, me).start()

    def permuted(f, k):
        return perm[f, pl.ds(k * repeat, repeat)].reshape(size, tokens)

    def back(t, l, k, value):
        f = step(t, l)
        rounded = (value * slope[f, k]).astype(BF16)
        scaled[f, k] = rounded
        work[0, work_rows(k), :] = dot(two_t[l, k], rounded)
        grad[k] = value
        product = value * silu[f, k]
        gate_acc[l, k] = product if t == 0 else gate_acc[l, k] + product

    def forward(t, l, then, early=None, late=None, low=0, high=CHUNKS):
        f = step(t, l)

        def chunk(c):
            for d in (1, 2, 3):
                copy_f(f, d, c, partner(d)).wait_recv()
            for b in range(per):
                k = c * per + b
                mixed = dot(two[l, k], permuted(f, k))
                logistic = 0.5 + 0.5 * jnp.tanh(0.5 * mixed)
                branch = mixed * logistic
                scale = gate_b[l, k]
                if l + 1 < slots:
                    old = hidden(t, l)[k].astype(F32)
                    new = jnp.where(l < count, old + scale * branch, old).astype(BF16)
                    hid[t, l, k] = new
                    work[room(t, l + 1), work_rows(k), :] = dot(one[l + 1, k], new)
                silu[f, k] = branch
                slope[f, k] = scale * (logistic * (1.0 + mixed * (1.0 - logistic)))
                if then is not None:
                    then(k)

        if low or high < CHUNKS:
            each_chunk(chunk, low, high)
        else:
            beside(chunk, early, late)

    def backward(t, l, then, early=None, late=None):
        f = step(t, l)

        def chunk(c):
            @pl.when(c == 0)
            def _():
                for d in (1, 2, 3):
                    copy_b(f, 0, d, c, partner(d)).wait_recv()

            for d in (1, 2, 3):
                copy_b(f, 1, d, c, partner(d)).wait_recv()
            for b in range(per):
                k = c * per + b
                term = dot(one_t[l, k], ret[f, k].reshape(size, tokens))
                value = jnp.where(l < count, grad[k] + term, grad[k])
                then(k, value)
                if t == 1 and l == 0:
                    first_grad(0, k)
            if t == 0 and l == 0:
                hop_send(c)

        beside(chunk, early, late)

    def hop_copy(c):
        part = pl.ds(c * per, per)
        return pltpu.make_async_remote_copy(
            src_ref=hop_out.at[part],
            dst_ref=hop_in.at[part],
            send_sem=hop_sent.at[c],
            recv_sem=hop_recv.at[c],
            device_id={"section": section - 1},
            device_id_type=MESH,
        )

    def hop_send(c):
        @pl.when(section > 0)
        def _():
            hop_copy(c).start()

    def second_grads(l):
        f, g = step(0, l), step(1, l)

        def block(k):
            left = jnp.concatenate([scaled[f, k], scaled[g, k]], axis=1)
            right = jnp.concatenate([permuted(f, k), permuted(g, k)], axis=1)
            total = lax.dot_general(left, right, (((1,), (1,)), ((), ())), preferred_element_type=F32)
            second_out[l, k] = jnp.where(l < count, total, 0.0).astype(BF16)
            gates = jnp.sum(gate_acc[l, k].T, axis=0, keepdims=True)
            gate_out[l, pl.ds(k, 1), :] = jnp.where(l < count, gates, 0.0)

        each_block(block)

    def first_grad(l, k):
            f, g = step(0, l), step(1, l)
            left = jnp.concatenate(
                [ret[f, k].reshape(size, tokens), ret[g, k].reshape(size, tokens)], axis=1
            )
            right = jnp.concatenate([hidden(0, l)[k], hidden(1, l)[k]], axis=1)
            total = lax.dot_general(left, right, (((1,), (1,)), ((), ())), preferred_element_type=F32)
            first_out[l, k] = jnp.where(l < count, total, 0.0).astype(BF16)

    def first_grads(l):
        each_block(functools.partial(first_grad, l))

    def start(t):
        def block(k):
            work[room(t, 0), work_rows(k), :] = dot(one[0, k], inp[t, k])

        each_block(block)

    def widen(l):
        def block(k):
            gate_b[l, k] = jnp.broadcast_to(gate[l, pl.ds(k, 1), :], (size, size)).T

        each_block(block)

    def turn_over(source, target, l):
        def block(k):
            target[l, k] = source[l, k].T

        each_block(block)

    load_inp(0).wait()
    load_one(0).wait()
    start(0)
    pl.semaphore_wait(
        barrier, 3 + jnp.where(section > 0, 1, 0) + jnp.where(section < last, 1, 0)
    )
    scatter_f(0, 0)
    load_inp(1).wait()
    start(1)
    load_gate.wait()
    widen(0)
    load_two(0).wait()

    half = CHUNKS // 2
    halves = [(0, half), (half, CHUNKS)]
    turns = [(l, h) for l in range(slots) for h in halves]

    def receive(n):
        if n <= 0:
            return None
        l, (low, high) = turns[n - 1]
        return lambda: forward(1, l, None, low=low, high=high)

    def send(n):
        l, (low, high) = turns[n]
        return lambda: scatter_f(1, l, low, high)

    def both(*calls):
        def run():
            for call in calls:
                if call is not None:
                    call()

        return run

    def ahead(t, l):
        return lambda: scatter_b(step(t, l), 0)

    top = slots - 1
    turn = 0
    for l in range(top):
        load_one(l + 1).wait()
        forward(0, l, None, receive(turn), send(turn))
        turn += 1
        scatter_f(0, l + 1)
        widen(l + 1)
        load_two(l + 1).wait()
    load_arr.wait()
    turn_over(two, two_t, top)
    forward(
        0, top, lambda k: back(0, top, k, arr[k].astype(F32)),
        both(ahead(0, top), receive(turn)), send(turn),
    )
    turn += 1
    scatter_b(step(0, top), 1)
    for l in range(top, 0, -1):
        turn_over(one, one_t, l)
        turn_over(two, two_t, l - 1)
        backward(
            0, l, functools.partial(back, 0, l - 1),
            both(ahead(0, l - 1), receive(turn)), send(turn),
        )
        turn += 1
        scatter_b(step(0, l - 1), 1)

    def leave(k, value):
        hop_out[k] = value.astype(BF16)

    turn_over(one, one_t, 0)
    backward(0, 0, leave, receive(turn), send(turn))
    turn += 1

    @pl.when(section == last)
    def _():
        pltpu.make_async_copy(loss, hop_in, loss_sem).wait()

    def arrive(c):
        @pl.when(section < last)
        def _():
            hop_copy(c).wait_recv()

        for b in range(per):
            k = c * per + b
            back(1, top, k, hop_in[k].astype(F32))

    beside(arrive, both(ahead(1, top), receive(turn)), None)
    scatter_b(step(1, top), 1)
    for l in range(top, 0, -1):
        second_grads(l)
        if l < top:
            first_grads(l + 1)
        backward(1, l, functools.partial(back, 1, l - 1), ahead(1, l - 1))
        scatter_b(step(1, l - 1), 1)
    second_grads(0)
    if top > 0:
        first_grads(1)

    def emit(k, value):
        emit_out[k] = value.astype(BF16)

    backward(1, 0, emit)

    for t in (0, 1):
        for l in range(slots):
            f = step(t, l)
            for d in (1, 2, 3):
                pltpu.make_async_remote_copy(
                    src_ref=send_f.at[f, d - 1], dst_ref=perm.at[f, :, me],
                    send_sem=sent_f.at[f, d - 1], recv_sem=recv_f.at[f, 0, d - 1],
                    device_id={"tensor": partner(d)}, device_id_type=MESH,
                ).wait_send()
                pltpu.make_async_remote_copy(
                    src_ref=send_b.at[f, d - 1], dst_ref=ret.at[f, :, me],
                    send_sem=sent_b.at[f, d - 1], recv_sem=recv_b.at[f, 0, d - 1],
                    device_id={"tensor": partner(d)}, device_id_type=MESH,
                ).wait_send()

    @pl.when(section > 0)
    def _():
        each_chunk(lambda c: hop_copy(c).wait_send())


def store_kernel(*refs):
    count = len(refs) // 2
    sems = refs[-1]
    copies = [
        pltpu.make_async_copy(refs[i], refs[count + i], sems.at[i]) for i in range(count)
    ]
    for copy in copies:
        copy.start()
    for copy in copies:
        copy.wait()


def store(values):
    return pl.pallas_call(
        store_kernel,
        out_shape=[jax.ShapeDtypeStruct(v.shape, v.dtype) for v in values],
        in_specs=[pl.BlockSpec(memory_space=pltpu.VMEM)] * len(values),
        out_specs=[pl.BlockSpec(memory_space=pl.ANY)] * len(values),
        scratch_shapes=[pltpu.SemaphoreType.DMA((len(values),))],
        compiler_params=pltpu.CompilerParams(vmem_limit_bytes=8 * 1024 * 1024),
    )(*values)


def fused_shards(
    section_inputs, arriving_grad, loss_grad, factor_first, factor_second, gate_scales, layer_count
):
    moments = section_inputs.shape[1]
    _, slots, blocks, size, _ = factor_first.shape
    tokens = section_inputs.shape[3]
    tensor = lax.axis_size("tensor")
    rows = size // tensor
    steps = moments * slots
    vmem = pl.BlockSpec(memory_space=pltpu.VMEM)
    block = (blocks, size, tokens)
    factor = (slots, blocks, size, size)
    outs = pl.pallas_call(
        kernel,
        out_shape=[
            pltpu.VMEM(block, BF16),
            pltpu.VMEM(factor, BF16),
            pltpu.VMEM(factor, BF16),
            pltpu.VMEM((slots, blocks, size), F32),
        ],
        in_specs=[pl.BlockSpec(memory_space=pl.ANY)] * 6 + [pl.BlockSpec(memory_space=pltpu.SMEM)],
        out_specs=[vmem] * 4,
        scratch_shapes=[
            pltpu.VMEM((moments,) + block, BF16),
            pltpu.VMEM(block, BF16),
            pltpu.VMEM(factor, BF16),
            pltpu.VMEM(factor, BF16),
            pltpu.VMEM(factor, BF16),
            pltpu.VMEM(factor, BF16),
            pltpu.VMEM((slots, blocks, size), F32),
            pltpu.VMEM((moments, max(slots - 1, 1)) + block, BF16),
            pltpu.VMEM((steps, rows, tensor, blocks, tokens), BF16),
            pltpu.VMEM((steps, blocks, tensor, 2, rows // 2, tokens), BF16),
            pltpu.VMEM((steps, 3, rows, blocks, tokens), BF16),
            pltpu.VMEM((steps, 3, blocks, 2, rows // 2, tokens), BF16),
            pltpu.VMEM((3, blocks * size, tokens), F32),
            pltpu.VMEM((steps,) + block, F32),
            pltpu.VMEM((steps,) + block, F32),
            pltpu.VMEM((slots,) + block, F32),
            pltpu.VMEM(block, F32),
            pltpu.VMEM((slots,) + block, F32),
            pltpu.VMEM((steps,) + block, BF16),
            pltpu.VMEM(block, BF16),
            pltpu.VMEM(block, BF16),
            pltpu.SemaphoreType.DMA((steps, CHUNKS, 3)),
            pltpu.SemaphoreType.DMA((steps, CHUNKS + 1, 3)),
            pltpu.SemaphoreType.DMA((steps, 3)),
            pltpu.SemaphoreType.DMA((steps, 3)),
            pltpu.SemaphoreType.DMA((CHUNKS,)),
            pltpu.SemaphoreType.DMA((CHUNKS,)),
            pltpu.SemaphoreType.DMA(()),
            pltpu.SemaphoreType.DMA((moments,)),
            pltpu.SemaphoreType.DMA((slots,)),
            pltpu.SemaphoreType.DMA((slots,)),
            pltpu.SemaphoreType.DMA((2,)),
        ],
        compiler_params=pltpu.CompilerParams(
            collective_id=0, has_side_effects=True, vmem_limit_bytes=56 * 1024 * 1024
        ),
    )(
        section_inputs[0].reshape((moments,) + block),
        arriving_grad[0].reshape(block),
        loss_grad[0].reshape(block),
        factor_first[0],
        factor_second[0],
        gate_scales[0].reshape(slots, blocks, size),
        layer_count,
    )
    emitted, first_grad, second_grad, gate_grad = store(outs)
    return (
        emitted.reshape(1, blocks * size, tokens),
        first_grad[None],
        second_grad[None],
        gate_grad.reshape(1, slots, blocks * size),
    )


def solution(mesh):
    in_specs = (
        P("section", None, "tensor", None),
        P("section", "tensor", None),
        P(None, "tensor", None),
        P("section", None, "tensor", None, None),
        P("section", None, "tensor", None, None),
        P("section", None, "tensor"),
        P("section"),
    )
    out_specs = (
        P("section", "tensor", None),
        P("section", None, "tensor", None, None),
        P("section", None, "tensor", None, None),
        P("section", None, "tensor"),
    )
    fused = mesh.shape["tensor"] == 4
    return jax.shard_map(fused_shards if fused else shards, mesh=mesh, in_specs=in_specs, out_specs=out_specs, check_vma=False)
```
